512 devices in a mesh: ctx: 64 (over z, y_lo, core), tp: 8 (over x, y_hi).
Axes of the slice: x: 4, y: 8 (y_hi: 2, y_lo: 4; y = y_hi * 4 + y_lo), z: 8, core: 2. Of those that a mesh axis runs over, the one named last changes fastest.
Arguments:
- hidden_in: bfloat16 [256, 8192], P('tp', 'ctx'), may hold values from -6 to 6
- w_query: bfloat16 [8192, 8192], P('ctx', 'tp'), may hold values from -0.1875 to 0.1875
- w_key: bfloat16 [8192, 1024], P('ctx', 'tp'), may hold values from -0.09375 to 0.09375
- w_value: bfloat16 [8192, 1024], P('ctx', 'tp'), may hold values from -0.09375 to 0.09375
- w_out: bfloat16 [8192, 8192], P('tp', 'ctx'), may hold values from -0.1875 to 0.1875
- cache_keys: bfloat16 [32768, 8, 128], P('ctx', 'tp'), may hold values from -512 to 512
- cache_values: bfloat16 [32768, 8, 128], P('ctx', 'tp'), may hold values from -6 to 6
- prefix_lengths: int32 [64], P('ctx'), may hold values from 1 to 512, as said below
Outputs:
- attention_out: float32 [256, 8192], P('tp', 'ctx')
The draws below stay inside these ranges and needn't reach their ends.
Inputs may be any that keep to these rules, and one draw needn't show every extreme that they name: `prefix_lengths`: every shard but the last holds 256 to 512 positions, and at least one of them is full; the last holds 1 to 512.
All inputs are finite; a program needn't handle non-finite values.
Results may differ from the reference program's by a relative error of at most 0.0059.
The reference program's roundings to bfloat16 on the way (of `query_proj`, `key_proj`, `weights` and `attended`) count: a program that leaves them out, or rounds other values in their place, can miss the bound.
Values may be sent and summed in bfloat16 or wider, within the bound.
A program may use at most 192 MiB of HBM per device.

```python
import jax
import jax.numpy as jnp
from jax import lax

D = 8192
HD = 128
GROUP = 8
SHARD = 512
KV_HEADS = 8
HEADS = 64
SPAN = 256
PREFIX = 32768
N_CTX = 64


def draw_cache_keys(key, part):
    key = jax.random.fold_in(key, 11)
    first = jax.random.fold_in(key, 0)
    values = jax.random.normal(first, (PREFIX, KV_HEADS, HD), jnp.float32)
    values = jnp.clip(values, -6.0, 6.0)
    return values.astype(jnp.bfloat16)


def draw_prefix_lengths(key, part):
    key = jax.random.fold_in(key, 5)
    first, second, third = jax.random.split(key, 3)
    lengths = jax.random.randint(first, (N_CTX,), SHARD // 2, SHARD + 1, jnp.int32)
    final = jax.random.randint(second, (), 1, SHARD + 1, jnp.int32)
    full_shard = jax.random.randint(third, (), 0, N_CTX - 1, jnp.int32)
    lengths = lengths.at[full_shard].set(SHARD)
    return lengths.at[N_CTX - 1].set(final)


def levels(own_key, extent, pieces, low, largest):
    def one(axis_at, shards_of):
        draws = jax.random.uniform(jax.random.fold_in(jax.random.fold_in(own_key, 6), axis_at), (shards_of,), jnp.float32, low / len(pieces), largest / len(pieces))
        return jnp.repeat(jnp.exp(draws), extent[axis_at] // shards_of).reshape((-1,) + (1,) * (len(extent) - axis_at - 1))

    gain = one(*pieces[0])
    for cut in pieces[1:]:
        gain = gain * one(*cut)
    return gain


def scatter_about(stream_key, extent, width, most, cuts=(), kind=jnp.bfloat16):
    loudness = levels(stream_key, extent, cuts, -0.22, 0.18) if cuts else 1.0
    values = jax.random.normal(stream_key, extent, jnp.float32) * width * loudness
    return jnp.minimum(jnp.maximum(values, -most), most).astype(kind)


def setup_inputs(seed: int = 0) -> dict:
    key_of = jax.random.split(jax.random.key(seed), 9)
    return {
        "hidden_in": scatter_about(key_of[0], (SPAN, D), 1.0, 6.0, ((0, 8), (1, 64))),
        "w_query": scatter_about(key_of[1], (D, HEADS * HD), (D // 8) ** -0.5, 0.1875, ((0, 64), (1, 8))),
        "w_key": scatter_about(key_of[2], (D, KV_HEADS * HD), (D // 2) ** -0.5, 0.09375, ((0, 64), (1, 8))),
        "w_value": scatter_about(key_of[3], (D, KV_HEADS * HD), (D // 2) ** -0.5, 0.09375, ((0, 64), (1, 8))),
        "w_out": scatter_about(key_of[4], (HEADS * HD, D), (HEADS * HD // 8) ** -0.5, 0.1875, ((0, 8), (1, 64))),
        "cache_keys": draw_cache_keys(jax.random.fold_in(key_of[8], 71), 0),
        "cache_values": scatter_about(key_of[6], (PREFIX, KV_HEADS, HD), 1.0, 6.0, ((0, 64), (1, 8))),
        "prefix_lengths": draw_prefix_lengths(jax.random.fold_in(key_of[8], 71), 0),
    }


def absorb(carried, queries, key_rows, value_rows, visible):
    weighted, highest, totals = carried
    scores = jnp.einsum("tkgd,skd->tkgs", queries, key_rows) * (HD ** -0.5)
    scores = jnp.where(visible, scores, -1e30)
    raised = jnp.maximum(highest, jnp.max(scores, axis=-1))
    shrink = jnp.exp(highest - raised)
    weights = jnp.exp(scores - raised[..., None])
    totals = totals * shrink + jnp.sum(weights, axis=-1)
    rounded = lax.optimization_barrier(weights.astype(jnp.bfloat16)).astype(jnp.float32)
    weighted = weighted * shrink[..., None] + jnp.einsum("tkgs,skd->tkgd", rounded, value_rows)
    return weighted, raised, totals


def reference(hidden_in, w_query, w_key, w_value, w_out, cache_keys, cache_values, prefix_lengths):
    query_proj = jnp.dot(hidden_in, w_query, preferred_element_type=jnp.float32).astype(jnp.bfloat16)
    key_proj = jnp.dot(hidden_in, w_key, preferred_element_type=jnp.float32).astype(jnp.bfloat16)
    value_proj = jnp.dot(hidden_in, w_value, preferred_element_type=jnp.float32).astype(jnp.bfloat16)
    queries = query_proj.astype(jnp.float32).reshape(SPAN, KV_HEADS, GROUP, HD)
    carried = (jnp.zeros((SPAN, KV_HEADS, GROUP, HD), jnp.float32),
               jnp.full((SPAN, KV_HEADS, GROUP), -1e30, jnp.float32),
               jnp.zeros((SPAN, KV_HEADS, GROUP), jnp.float32))
    key_shards = cache_keys.reshape(N_CTX, SHARD, KV_HEADS, HD)
    value_shards = cache_values.reshape(N_CTX, SHARD, KV_HEADS, HD)
    offsets = jnp.arange(SHARD, dtype=jnp.int32)

    def advance(status, inputs):
        key_rows, value_rows, filled = inputs
        visible = (offsets < filled)[None, None, None, :]
        return absorb(status, queries, key_rows.astype(jnp.float32), value_rows.astype(jnp.float32), visible), None

    carried, unused = lax.scan(advance, carried, (key_shards, value_shards, prefix_lengths))
    tokens = jnp.arange(SPAN, dtype=jnp.int32)
    causal = (tokens[None, :] <= tokens[:, None])[:, None, None, :]
    carried = absorb(carried, queries, key_proj.astype(jnp.float32).reshape(SPAN, KV_HEADS, HD),
                     value_proj.astype(jnp.float32).reshape(SPAN, KV_HEADS, HD), causal)
    weighted, highest, totals = carried
    attended = (weighted / totals[..., None]).astype(jnp.bfloat16).reshape(SPAN, HEADS * HD)
    return jnp.dot(attended, w_out, preferred_element_type=jnp.float32)
```

```python
import functools
import math

import jax
import jax.numpy as jnp
from jax import lax
from jax.experimental import pallas as pl
from jax.experimental.pallas import tpu as pltpu
from jax.sharding import PartitionSpec as P

MESH = pl.DeviceIdType.MESH
F32 = jnp.float32
BF16 = jnp.bfloat16
NZ, NY, NX, NH = 8, 4, 4, 2
LOG2E = 1.0 / math.log(2.0)
NEG = -1e30


def coords():
    c = lax.axis_index("ctx")
    t = lax.axis_index("tp")
    return c // 8, (c // 2) % 4, c % 2, t // 2, t % 2


def device(z, y, core, x, h):
    return ((z * NY + y) * 2 + core, x * NH + h)


def dot(a, b):
    return jnp.dot(a, b, preferred_element_type=F32)


def dot_t(a, b):
    return lax.dot_general(a, b, (((1,), (1,)), ((), ())), preferred_element_type=F32)


def kernel(
    hid_ref, wq_ref, wk_ref, wv_ref, wo_ref, ck_ref, cv_ref, len_ref, out_ref,
    hs, wq, wkv, wo, kb, vb, yp, yin, kvs, kvin, p2s, p2d, qb, msgs, m_s, l_s, acc,
    po, pl_s, pod, pld, att, o2s, p7,
    loc, s_hy, r_hy, s_hx, r_hx, s_w, r_w, s_wo, r_wo, s_kc, r_kc, s_ky, r_ky, s_kr, r_kr,
    s_pc, r_pc, s_p2, r_p2, s_p3, r_p3, s_m, r_m, s_p5, r_p5, s_p6, r_p6, s_rc, r_rc, s_p7, r_p7,
):
    z, y, core, x, h = coords()
    other = 1 - core
    yf = h * NY + y
    tp = x * NH + h
    mine = y * 2 + core

    def remote(src, dst, ssem, rsem, dev):
        return pltpu.make_async_remote_copy(
            src_ref=src, dst_ref=dst, send_sem=ssem, recv_sem=rsem, device_id=dev, device_id_type=MESH
        )

    sends = []

    local = [
        pltpu.make_async_copy(wq_ref.at[:, pl.ds(pl.multiple_of(y * 256, 256), 256)], wq.at[y], loc.at[0]),
        pltpu.make_async_copy(wo_ref.at[pl.ds(pl.multiple_of(y * 256, 256), 256)], wo.at[y], loc.at[1]),
        pltpu.make_async_copy(ck_ref, kb.at[mine], loc.at[2]),
        pltpu.make_async_copy(cv_ref, vb.at[mine], loc.at[3]),
    ]
    for copy in local:
        copy.start()

    barrier = pltpu.get_barrier_semaphore()

    def greet(i, carry):
        dev = device(z, lax.rem(y + i % 4, 4), core, lax.rem(x + i // 8, 4), lax.rem(h + (i // 4) % 2, 2))
        pl.semaphore_signal(barrier, inc=1, device_id=dev, device_id_type=MESH)
        return carry

    lax.fori_loop(1, 32, greet, 0)
    for d in range(1, NZ):
        pl.semaphore_signal(
            barrier, inc=1, device_id=device(lax.rem(z + d, NZ), y, core, x, h), device_id_type=MESH
        )
    for d in range(NY):
        pl.semaphore_signal(
            barrier, inc=1, device_id=device(z, lax.rem(y + d, NY), other, x, h), device_id_type=MESH
        )
    pl.semaphore_wait(barrier, 31 + NZ - 1 + NY)

    own_rows = pl.ds(pl.multiple_of(tp * 32, 32), 32)
    own_cols = pl.ds(pl.multiple_of(y * 128, 128), 128)

    def hid_y(d):
        to = lax.rem(yf + d, 8)
        return remote(hid_ref, hs.at[own_rows, own_cols], s_hy.at[d], r_hy.at[d], device(z, to % 4, core, x, to // 4))

    for d in range(1, 8):
        copy = hid_y(d)
        copy.start()
        sends.append(copy)
    hs[own_rows, own_cols] = hid_ref[...]

    def weights(d):
        to = lax.rem(y + d, NY)
        dev = device(z, to, core, x, h)
        first = remote(
            wq_ref.at[:, pl.ds(pl.multiple_of(to * 256, 256), 256)], wq.at[y], s_w.at[0, d], r_w.at[0, d], dev
        )
        return first, to, dev

    def weights_kv(ref, d, dev):
        return remote(ref, wkv.at[y], s_w.at[1, d], r_w.at[1, d], dev)

    for d in range(1, NY):
        first, to, dev = weights(d)
        first.start()
        sends.append(first)

        @pl.when(to % 2 == 0)
        def _():
            weights_kv(wk_ref, d, dev).start()

        @pl.when(to % 2 == 1)
        def _():
            weights_kv(wv_ref, d, dev).start()

        sends.append(weights_kv(wk_ref, d, dev))

    @pl.when(y % 2 == 0)
    def _():
        wkv[y] = wk_ref[...]

    @pl.when(y % 2 == 1)
    def _():
        wkv[y] = wv_ref[...]

    twin = device(z, y, other, x, h)
    for i, (ref, buf) in enumerate(((ck_ref, kb), (cv_ref, vb))):
        copy = remote(ref, buf.at[mine], s_kc.at[i], r_kc.at[i], twin)
        copy.start()
        sends.append(copy)

    for d in range(1, 8):
        hid_y(d).wait_recv()

    def hid_x(d):
        rows = pl.ds(pl.multiple_of(x * 64, 64), 64)
        return remote(hs.at[rows], hs.at[rows], s_hx.at[d], r_hx.at[d], device(z, y, core, lax.rem(x + d, NX), h))

    for d in range(1, NX):
        copy = hid_x(d)
        copy.start()
        sends.append(copy)

    for d in range(1, NY):
        first, to, dev = weights(d)
        first.wait_recv()
        weights_kv(wk_ref, d, dev).wait_recv()
    local[0].wait()

    def cache_y(d, i):
        ref, buf = ((ck_ref, kb), (cv_ref, vb))[i]
        return remote(ref, buf.at[mine], s_ky.at[i, d], r_ky.at[i, d], device(z, lax.rem(y + d, NY), core, x, h))

    for d in (1, 3, 2):
        for i in range(2):
            copy = cache_y(d, i)
            copy.start()
            sends.append(copy)

    def out_weights(d):
        to = lax.rem(y + d, NY)
        return remote(
            wo_ref.at[pl.ds(pl.multiple_of(to * 256, 256), 256)], wo.at[y], s_wo.at[d], r_wo.at[d],
            device(z, to, core, x, h),
        )

    for d in range(1, NY):
        copy = out_weights(d)
        copy.start()
        sends.append(copy)

    wqf = wq[...].reshape(512, 256)
    wkvf = wkv[...].reshape(512, 128)

    def project(block):
        rows = pl.ds(pl.multiple_of(block * 64, 64), 64)
        part = hs[rows, :]
        both = dot(part, wqf)
        yp[0, rows, :] = both[:, :128]
        yp[1, rows, :] = both[:, 128:]
        yp[2, rows, :] = dot(part, wkvf)

    project(x)
    for d in range(1, NX):
        hid_x(d).wait_recv()
        project(lax.rem(x + NX - d, NX))

    half = 16 * (y // 2)
    for b in range(NZ):
        kvs[b] = yp[2, pl.ds(pl.multiple_of(32 * b + half + 8 * other, 8), 8), :]
    pair = [
        remote(yp.at[other], yin, s_pc.at[0], r_pc.at[0], twin),
        remote(kvs, kvin, s_pc.at[1], r_pc.at[1], twin),
    ]
    for copy in pair:
        copy.start()
        sends.append(copy)
    for copy in pair:
        copy.wait_recv()
    for b in range(NZ):
        rows = slice(32 * b, 32 * b + 32)
        p2s[b, 0:32, :] = yp[core, rows, :] + yin[rows, :]
        p2s[b, 32:40, :] = yp[2, pl.ds(pl.multiple_of(32 * b + half + 8 * core, 8), 8), :] + kvin[b]

    def zdev(d):
        to = lax.rem(z + d, NZ)
        return to, device(to, y, core, x, h)

    def p2(d):
        to, dev = zdev(d)
        return remote(p2s.at[to], p2d.at[z], s_p2.at[d], r_p2.at[d], dev)

    for d in range(1, NZ):
        copy = p2(d)
        copy.start()
        sends.append(copy)
    p2d[z] = p2s[z]
    for d in range(1, NZ):
        p2(d).wait_recv()
    total = p2d[0]
    for b in range(1, NZ):
        total = total + p2d[b]
    zrows = pl.ds(pl.multiple_of(z * 32, 32), 32)
    qb[zrows, :] = total[:32].astype(BF16)

    def p3(d):
        to, dev = zdev(d)
        return remote(qb.at[zrows], qb.at[zrows], s_p3.at[d], r_p3.at[d], dev)

    for d in range(1, NZ):
        copy = p3(d)
        copy.start()
        sends.append(copy)

    msgs[mine, 0:8, :] = total[32:]
    msgs[mine, 8:16, :] = jnp.full((8, 128), len_ref[0].astype(F32), F32)

    def message(d, k):
        dev = device(z, lax.rem(y + d, NY), lax.rem(core + k, 2), x, h)
        return remote(msgs.at[mine], msgs.at[mine], s_m.at[k, d], r_m.at[k, d], dev)

    line = [(d, k) for d in range(NY) for k in range(2) if (d, k) != (0, 0)]
    for d, k in line:
        copy = message(d, k)
        copy.start()
        sends.append(copy)
    for d, k in line:
        message(d, k).wait_recv()
    for d in range(1, NZ):
        p3(d).wait_recv()

    scale = LOG2E / math.sqrt(128.0)
    queries = qb[...]
    m_s[...] = jnp.full((256, 1), NEG, F32)
    l_s[...] = jnp.zeros((256, 1), F32)
    acc[...] = jnp.zeros((256, 128), F32)

    def absorb(scores, values):
        before = m_s[...]
        raised = jnp.maximum(before, jnp.max(scores, axis=1, keepdims=True))
        shrink = jnp.exp2(before - raised)
        weight = jnp.exp2(scores - raised)
        l_s[...] = l_s[...] * shrink + jnp.sum(weight, axis=1, keepdims=True)
        acc[...] = acc[...] * shrink + dot(weight.astype(BF16), values)
        m_s[...] = raised

    def shard(index):
        filled = jnp.concatenate([msgs[index, 8:9, :]] * 4, axis=1)
        place = lax.broadcasted_iota(jnp.int32, (1, 512), 1).astype(F32)
        bias = jnp.where(place < filled, 0.0, NEG)
        absorb(dot_t(queries, kb[index]) * scale + bias, vb[index])

    def relay(d, i):
        index = lax.rem(y + NY - d, NY) * 2 + core
        buf = (kb, vb)[i]
        return remote(buf.at[index], buf.at[index], s_kr.at[i, d], r_kr.at[i, d], twin)

    local[2].wait()
    local[3].wait()
    shard(mine)
    for i, (ref, buf) in enumerate(((ck_ref, kb), (cv_ref, vb))):
        remote(ref, buf.at[mine], s_kc.at[i], r_kc.at[i], twin).wait_recv()
    shard(y * 2 + other)

    new_keys = jnp.concatenate([msgs[i, 0:8, :] for i in (0, 1, 4, 5)], axis=0).astype(BF16)
    new_values = jnp.concatenate([msgs[i, 0:8, :] for i in (2, 3, 6, 7)], axis=0).astype(BF16)
    key_at = lax.broadcasted_iota(jnp.int32, (256, 32), 1) + z * 32
    row_at = lax.broadcasted_iota(jnp.int32, (256, 32), 0)
    absorb(jnp.where(key_at <= row_at, dot_t(queries, new_keys) * scale, NEG), new_values)

    for d in (1, 3, 2):
        for i in range(2):
            cache_y(d, i).wait_recv()
            copy = relay(d, i)
            copy.start()
            sends.append(copy)
        shard(lax.rem(y + NY - d, NY) * 2 + core)
        for i in range(2):
            relay(d, i).wait_recv()
        shard(lax.rem(y + NY - d, NY) * 2 + other)

    sums = l_s[...]
    po[...] = (acc[...] / sums).astype(BF16)
    level = m_s[...] + jnp.log2(sums)
    diagonal = lax.broadcasted_iota(jnp.int32, (32, 128), 0) == lax.broadcasted_iota(jnp.int32, (32, 128), 1)
    for b in range(NZ):
        spread = jnp.where(diagonal, level[32 * b : 32 * b + 32], 0.0)
        pl_s[b] = jnp.broadcast_to(jnp.sum(spread, axis=0, keepdims=True), (8, 128))

    def p5(d, i):
        to, dev = zdev(d)
        if i == 0:
            rows = pl.ds(pl.multiple_of(to * 32, 32), 32)
            return remote(po.at[rows], pod.at[z], s_p5.at[0, d], r_p5.at[0, d], dev)
        return remote(pl_s.at[to], pld.at[z], s_p5.at[1, d], r_p5.at[1, d], dev)

    for d in range(1, NZ):
        for i in range(2):
            copy = p5(d, i)
            copy.start()
            sends.append(copy)
    pod[z] = po[zrows, :]
    pld[z] = pl_s[z]
    for d in range(1, NZ):
        for i in range(2):
            p5(d, i).wait_recv()

    levels = []
    for b in range(NZ):
        spread = jnp.where(diagonal, jnp.broadcast_to(pld[b, 0:1, :], (32, 128)), 0.0)
        levels.append(jnp.sum(spread, axis=1, keepdims=True))
    top = functools.reduce(jnp.maximum, levels)
    shares = [jnp.exp2(level_b - top) for level_b in levels]
    whole = functools.reduce(jnp.add, shares)
    merged = functools.reduce(jnp.add, [pod[b].astype(F32) * shares[b] for b in range(NZ)])
    att[0, zrows, :] = (merged / whole).astype(BF16)

    def p6(d):
        to, dev = zdev(d)
        return remote(att.at[0, zrows], att.at[0, zrows], s_p6.at[d], r_p6.at[d], dev)

    for d in range(1, NZ):
        copy = p6(d)
        copy.start()
        sends.append(copy)
    for d in range(1, NZ):
        p6(d).wait_recv()
    across = remote(att.at[0], att.at[1], s_rc, r_rc, twin)
    across.start()
    sends.append(across)

    local[1].wait()
    for d in range(1, NY):
        out_weights(d).wait_recv()
    head_rows = pl.ds(pl.multiple_of(core * 128, 128), 128)
    twin_rows = pl.ds(pl.multiple_of(other * 128, 128), 128)
    first = [dot(att[0], wo[b, head_rows, :]) for b in range(NY)]
    across.wait_recv()
    for b in range(NY):
        o2s[b] = (first[b] + dot(att[1], wo[b, twin_rows, :])).astype(BF16)

    def p7_copy(i):
        ty, tx, th = lax.rem(y + i % 4, 4), lax.rem(x + i // 8, 4), lax.rem(h + (i // 4) % 2, 2)
        rows = pl.ds(pl.multiple_of((tx * NH + th) * 32, 32), 32)
        return remote(
            o2s.at[ty, rows], p7.at[tp * NY + y], s_p7.at[i], r_p7.at[i], device(z, ty, core, tx, th)
        )

    def p7_start(i, carry):
        p7_copy(i).start()
        return carry

    def p7_recv(i, carry):
        p7_copy(i).wait_recv()
        return carry

    def p7_send(i, carry):
        p7_copy(i).wait_send()
        return carry

    lax.fori_loop(1, 32, p7_start, 0)
    p7[tp * NY + y] = o2s[y, own_rows, :]
    lax.fori_loop(1, 32, p7_recv, 0)
    result = p7[0].astype(F32)
    for b in range(1, 32):
        result = result + p7[b].astype(F32)
    out_ref[...] = result

    for copy in sends:
        copy.wait_send()
    lax.fori_loop(1, 32, p7_send, 0)


def per_device(hidden_in, w_query, w_key, w_value, w_out, cache_keys, cache_values, prefix_lengths):
    dma = pltpu.SemaphoreType.DMA
    vmem = pltpu.VMEM
    in_vmem = pl.BlockSpec(memory_space=pltpu.VMEM)
    anywhere = pl.BlockSpec(memory_space=pl.ANY)
    return pl.pallas_call(
        kernel,
        out_shape=jax.ShapeDtypeStruct((32, 128), F32),
        in_specs=[in_vmem, anywhere, in_vmem, in_vmem, anywhere, anywhere, anywhere,
                  pl.BlockSpec(memory_space=pltpu.SMEM)],
        out_specs=in_vmem,
        scratch_shapes=[
            vmem((256, 512), BF16), vmem((4, 128, 256), BF16), vmem((4, 128, 128), BF16),
            vmem((4, 256, 128), BF16), vmem((8, 512, 128), BF16), vmem((8, 512, 128), BF16),
            vmem((3, 256, 128), F32), vmem((256, 128), F32), vmem((8, 8, 128), F32), vmem((8, 8, 128), F32),
            vmem((8, 40, 128), F32), vmem((8, 40, 128), F32), vmem((256, 128), BF16), vmem((8, 16, 128), F32),
            vmem((256, 1), F32), vmem((256, 1), F32), vmem((256, 128), F32),
            vmem((256, 128), BF16), vmem((8, 8, 128), F32), vmem((8, 32, 128), BF16), vmem((8, 8, 128), F32),
            vmem((2, 256, 128), BF16), vmem((4, 256, 128), BF16), vmem((32, 32, 128), BF16),
            dma((4,)), dma((8,)), dma((8,)), dma((4,)), dma((4,)), dma((2, 4)), dma((2, 4)), dma((4,)), dma((4,)),
            dma((2,)), dma((2,)), dma((2, 4)), dma((2, 4)), dma((2, 4)), dma((2, 4)),
            dma((2,)), dma((2,)), dma((8,)), dma((8,)), dma((8,)), dma((8,)), dma((2, 4)), dma((2, 4)),
            dma((2, 8)), dma((2, 8)), dma((8,)), dma((8,)), dma, dma, dma((32,)), dma((32,)),
        ],
        compiler_params=pltpu.CompilerParams(
            collective_id=0, has_side_effects=True, vmem_limit_bytes=40 * 1024 * 1024
        ),
        cost_estimate=pl.CostEstimate(flops=1_000_000_000, bytes_accessed=2_000_000, transcendentals=1_100_000),
        name="attention_block",
    )(
        hidden_in, w_query, w_key, w_value, w_out,
        cache_keys.reshape(cache_keys.shape[0], 128), cache_values.reshape(cache_values.shape[0], 128),
        prefix_lengths,
    )


def solution(mesh):
    placed = (
        P("tp", "ctx"),
        P("ctx", "tp"),
        P("ctx", "tp"),
        P("ctx", "tp"),
        P("tp", "ctx"),
        P("ctx", "tp", None),
        P("ctx", "tp", None),
        P("ctx"),
    )
    return jax.shard_map(
        per_device, mesh=mesh, in_specs=placed, out_specs=P("tp", "ctx"), check_vma=False
    )
```

```python
import functools
import math

import jax
import jax.numpy as jnp
from jax import lax
from jax.experimental import pallas as pl
from jax.experimental.pallas import tpu as pltpu
from jax.sharding import PartitionSpec as P

MESH = pl.DeviceIdType.MESH
F32 = jnp.float32
BF16 = jnp.bfloat16
NZ, NY, NX, NH = 8, 4, 4, 2
LOG2E = 1.0 / math.log(2.0)
NEG = -1e30
KEYS_WITH = 1
HEADS_WITH = 2


def coords():
    c = lax.axis_index("ctx")
    t = lax.axis_index("tp")
    return c // 8, (c // 2) % 4, c % 2, t // 2, t % 2


def device(z, y, core, x, h):
    return ((z * NY + y) * 2 + core, x * NH + h)


def dot(a, b):
    return jnp.dot(a, b, preferred_element_type=F32)


def dot_t(a, b):
    return lax.dot_general(a, b, (((1,), (1,)), ((), ())), preferred_element_type=F32)


def kernel(
    hid_ref, wq_ref, wk_ref, wv_ref, wo_ref, ck_ref, cv_ref, len_ref, out_ref,
    hs, wqs, wkvs, wos, wq, wkv, wo, kb, vb, yp, yin, kvs, kvin, p2s, p2d, qb, msgs, m_s, l_s, acc,
    po, pod, att, o2s, p7,
    loc, s_hy, r_hy, s_hx, r_hx, s_w, r_w, s_wo, r_wo, s_kc, r_kc, s_ky, r_ky, s_kr, r_kr,
    s_pc, r_pc, s_p2, r_p2, s_p3, r_p3, s_m, r_m, s_p5, r_p5, s_p6, r_p6, s_rc, r_rc, s_p7, r_p7,
):
    z, y, core, x, h = coords()
    other = 1 - core
    yf = h * NY + y
    tp = x * NH + h
    mine = y * 2 + core
    own_rows = pl.ds(pl.multiple_of(tp * 32, 32), 32)
    own_cols = pl.ds(pl.multiple_of(y * 128, 128), 128)

    def xor_y(bits):
        if bits == 1:
            return y + 1 - 2 * (y % 2)
        return lax.rem(y + 2, NY)

    keys_y, heads_y = xor_y(KEYS_WITH), xor_y(HEADS_WITH)

    def remote(src, dst, ssem, rsem, dev):
        return pltpu.make_async_remote_copy(
            src_ref=src, dst_ref=dst, send_sem=ssem, recv_sem=rsem, device_id=dev, device_id_type=MESH
        )

    sends = []

    local = [
        pltpu.make_async_copy(hid_ref, hs.at[own_rows, own_cols], loc.at[0]),
        pltpu.make_async_copy(wq_ref, wqs, loc.at[1]),
        pltpu.make_async_copy(wk_ref, wkvs.at[0], loc.at[2]),
        pltpu.make_async_copy(wv_ref, wkvs.at[1], loc.at[3]),
        pltpu.make_async_copy(ck_ref, kb.at[mine], loc.at[4]),
        pltpu.make_async_copy(cv_ref, vb.at[mine], loc.at[5]),
        pltpu.make_async_copy(wo_ref, wos, loc.at[6]),
    ]
    for copy in local:
        copy.start()

    barrier = pltpu.get_barrier_semaphore()

    def greet(i, carry):
        dev = device(z, lax.rem(y + i % 4, 4), core, lax.rem(x + i // 8, 4), lax.rem(h + (i // 4) % 2, 2))
        pl.semaphore_signal(barrier, inc=1, device_id=dev, device_id_type=MESH)
        return carry

    lax.fori_loop(1, 32, greet, 0)
    for d in range(1, NZ):
        pl.semaphore_signal(
            barrier, inc=1, device_id=device(lax.rem(z + d, NZ), y, core, x, h), device_id_type=MESH
        )
        pl.semaphore_signal(
            barrier, inc=1, device_id=device(lax.rem(z + d, NZ), heads_y, core, x, h), device_id_type=MESH
        )
    for d in range(NY):
        pl.semaphore_signal(
            barrier, inc=1, device_id=device(z, lax.rem(y + d, NY), other, x, h), device_id_type=MESH
        )
    pl.semaphore_wait(barrier, 31 + 2 * (NZ - 1) + NY)

    own_hidden = hs.at[own_rows, own_cols]

    def hid_y(d):
        to = lax.rem(yf + d, 8)
        return remote(own_hidden, own_hidden, s_hy.at[d], r_hy.at[d], device(z, to % 4, core, x, to // 4))

    local[0].wait()
    for d in range(1, 8):
        copy = hid_y(d)
        copy.start()
        sends.append(copy)

    def weights(d, i):
        to = lax.rem(y + d, NY)
        dev = device(z, to, core, x, h)
        if i == 0:
            part = wqs.at[:, pl.ds(pl.multiple_of(to * 256, 256), 256)]
            return remote(part, wq.at[y], s_w.at[0, d], r_w.at[0, d], dev)
        return remote(wkvs.at[to % 2], wkv.at[y], s_w.at[1, d], r_w.at[1, d], dev)

    for copy in local[1:4]:
        copy.wait()
    for d in range(1, NY):
        for i in range(2):
            copy = weights(d, i)
            copy.start()
            sends.append(copy)
    wq[y] = wqs[:, pl.ds(pl.multiple_of(y * 256, 256), 256)]
    wkv[y] = wkvs[y % 2]

    twin = device(z, y, other, x, h)

    def cache_twin(i):
        buf = (kb, vb)[i]
        return remote(buf.at[mine], buf.at[mine], s_kc.at[i], r_kc.at[i], twin)

    for i in range(2):
        local[4 + i].wait()
        copy = cache_twin(i)
        copy.start()
        sends.append(copy)

    for d in range(1, 8):
        hid_y(d).wait_recv()

    def hid_x(d):
        rows = pl.ds(pl.multiple_of(x * 64, 64), 64)
        return remote(hs.at[rows], hs.at[rows], s_hx.at[d], r_hx.at[d], device(z, y, core, lax.rem(x + d, NX), h))

    for d in range(1, NX):
        copy = hid_x(d)
        copy.start()
        sends.append(copy)

    for d in range(1, NY):
        for i in range(2):
            weights(d, i).wait_recv()

    def cache_y(i):
        buf = (kb, vb)[i]
        return remote(buf.at[mine], buf.at[mine], s_ky.at[i], r_ky.at[i], device(z, keys_y, core, x, h))

    for i in range(2):
        copy = cache_y(i)
        copy.start()
        sends.append(copy)

    def out_weights(d):
        to = lax.rem(y + d, NY)
        return remote(
            wos.at[pl.ds(pl.multiple_of(to * 256, 256), 256)], wo.at[y], s_wo.at[d], r_wo.at[d],
            device(z, to, core, x, h),
        )

    local[6].wait()
    for d in range(1, NY):
        copy = out_weights(d)
        copy.start()
        sends.append(copy)
    wo[y] = wos[pl.ds(pl.multiple_of(y * 256, 256), 256), :]

    wqf = wq[...].reshape(512, 256)
    wkvf = wkv[...].reshape(512, 128)

    def project(block):
        rows = pl.ds(pl.multiple_of(block * 64, 64), 64)
        part = hs[rows, :]
        both = dot(part, wqf)
        yp[0, rows, :] = both[:, :128]
        yp[1, rows, :] = both[:, 128:]
        yp[2, rows, :] = dot(part, wkvf)

    project(x)
    for d in range(1, NX):
        hid_x(d).wait_recv()
        project(lax.rem(x + NX - d, NX))

    half = 16 * (y // 2)
    for b in range(NZ):
        kvs[b] = yp[2, pl.ds(pl.multiple_of(32 * b + half + 8 * other, 8), 8), :]
    pair = [
        remote(yp.at[other], yin, s_pc.at[0], r_pc.at[0], twin),
        remote(kvs, kvin, s_pc.at[1], r_pc.at[1], twin),
    ]
    for copy in pair:
        copy.start()
        sends.append(copy)
    for copy in pair:
        copy.wait_recv()
    for b in range(NZ):
        rows = slice(32 * b, 32 * b + 32)
        p2s[b, 0:32, :] = yp[core, rows, :] + yin[rows, :]
        p2s[b, 32:40, :] = yp[2, pl.ds(pl.multiple_of(32 * b + half + 8 * core, 8), 8), :] + kvin[b]

    def zdev(d):
        to = lax.rem(z + d, NZ)
        return to, device(to, y, core, x, h)

    def p2(d):
        to, dev = zdev(d)
        return remote(p2s.at[to], p2d.at[z], s_p2.at[d], r_p2.at[d], dev)

    for d in range(1, NZ):
        copy = p2(d)
        copy.start()
        sends.append(copy)
    p2d[z] = p2s[z]
    for d in range(1, NZ):
        p2(d).wait_recv()
    total = p2d[0]
    for b in range(1, NZ):
        total = total + p2d[b]
    zrows = pl.ds(pl.multiple_of(z * 32, 32), 32)
    qb[0, zrows, :] = total[:32].astype(BF16)

    def zdev2(d, j):
        to = lax.rem(z + d, NZ)
        return to, device(to, (y, heads_y)[j], core, x, h)

    def p3(d, j):
        to, dev = zdev2(d, j)
        return remote(qb.at[0, zrows], qb.at[j, zrows], s_p3.at[j, d], r_p3.at[j, d], dev)

    pairs = [(d, j) for d in (4, 3, 5, 2, 6, 1, 7, 0) for j in (1, 0) if (d, j) != (0, 0)]
    for d, j in pairs:
        copy = p3(d, j)
        copy.start()
        sends.append(copy)

    msgs[mine, 0:8, :] = total[32:]
    msgs[mine, 8:16, :] = jnp.full((8, 128), len_ref[0].astype(F32), F32)

    def message(d, k):
        dev = device(z, lax.rem(y + d, NY), lax.rem(core + k, 2), x, h)
        return remote(msgs.at[mine], msgs.at[mine], s_m.at[k, d], r_m.at[k, d], dev)

    line = [(d, k) for d in range(NY) for k in range(2) if (d, k) != (0, 0)]
    for d, k in line:
        copy = message(d, k)
        copy.start()
        sends.append(copy)
    for d, j in pairs:
        p3(d, j).wait_recv()

    scale = LOG2E / math.sqrt(128.0)
    queries = qb[...].reshape(512, 128)
    m_s[...] = jnp.full((512, 1), NEG, F32)
    l_s[...] = jnp.zeros((512, 1), F32)
    acc[...] = jnp.zeros((512, 128), F32)

    def absorb(rows, scores, values):
        before = m_s[0:rows]
        raised = jnp.maximum(before, jnp.max(scores, axis=1, keepdims=True))
        shrink = jnp.exp2(before - raised)
        weight = jnp.exp2(scores - raised)
        l_s[0:rows] = l_s[0:rows] * shrink + jnp.sum(weight, axis=1, keepdims=True)
        acc[0:rows] = acc[0:rows] * shrink + dot(weight.astype(BF16), values)
        m_s[0:rows] = raised

    def shard(index):
        filled = jnp.concatenate([msgs[index, 8:9, :]] * 4, axis=1)
        place = lax.broadcasted_iota(jnp.int32, (1, 512), 1).astype(F32)
        bias = jnp.where(place < filled, 0.0, NEG)
        absorb(512, dot_t(queries, kb[index]) * scale + bias, vb[index])

    def relay(i):
        index = keys_y * 2 + core
        buf = (kb, vb)[i]
        return remote(buf.at[index], buf.at[index], s_kr.at[i], r_kr.at[i], twin)

    for i in range(2):
        cache_y(i).wait_recv()
        copy = relay(i)
        copy.start()
        sends.append(copy)
    shard(mine)
    for d, k in line:
        message(d, k).wait_recv()
    for i in range(2):
        cache_twin(i).wait_recv()
    shard(y * 2 + other)
    shard(keys_y * 2 + core)

    new_keys = jnp.concatenate([msgs[i, 0:8, :] for i in (0, 1, 4, 5)], axis=0).astype(BF16)
    new_values = jnp.concatenate([msgs[i, 0:8, :] for i in (2, 3, 6, 7)], axis=0).astype(BF16)
    key_at = lax.broadcasted_iota(jnp.int32, (256, 32), 1) + z * 32
    row_at = lax.broadcasted_iota(jnp.int32, (256, 32), 0)
    absorb(256, jnp.where(key_at <= row_at, dot_t(queries[:256], new_keys) * scale, NEG), new_values)

    for i in range(2):
        relay(i).wait_recv()
    shard(keys_y * 2 + other)

    sums = l_s[...]
    shared = (acc[...] / sums).astype(BF16)
    level = m_s[...] + jnp.log2(sums)
    diagonal = lax.broadcasted_iota(jnp.int32, (32, 128), 0) == lax.broadcasted_iota(jnp.int32, (32, 128), 1)
    row16 = lax.broadcasted_iota(jnp.int32, (16, 128), 0)
    for j in range(2):
        for b in range(NZ):
            rows = slice(256 * j + 32 * b, 256 * j + 32 * b + 32)
            po[j, b, 0:32, :] = shared[rows]
            line_of = jnp.sum(jnp.where(diagonal, level[rows], 0.0), axis=0, keepdims=True)
            high = line_of.astype(BF16).astype(F32)
            mid = (line_of - high).astype(BF16).astype(F32)
            low = line_of - high - mid
            po[j, b, 32:48, :] = jnp.where(row16 == 0, high, jnp.where(row16 == 1, mid, low)).astype(BF16)

    def p5(d, j):
        to, dev = zdev2(d, j)
        return remote(po.at[j, to], pod.at[j, z], s_p5.at[j, d], r_p5.at[j, d], dev)

    for d, j in pairs:
        copy = p5(d, j)
        copy.start()
        sends.append(copy)
    pod[0, z] = po[0, z]
    for d, j in pairs:
        p5(d, j).wait_recv()

    levels, parts = [], []
    for j in range(2):
        for b in range(NZ):
            rows = pod[j, b, 32:48, :].astype(F32)
            line_of = rows[0:1] + rows[1:2] + rows[2:3]
            spread = jnp.where(diagonal, jnp.broadcast_to(line_of, (32, 128)), 0.0)
            levels.append(jnp.sum(spread, axis=1, keepdims=True))
            parts.append(pod[j, b, 0:32, :].astype(F32))
    top = functools.reduce(jnp.maximum, levels)
    shares = [jnp.exp2(one - top) for one in levels]
    whole = functools.reduce(jnp.add, shares)
    merged = functools.reduce(jnp.add, [part * share for part, share in zip(parts, shares)])
    att[0, zrows, :] = (merged / whole).astype(BF16)

    def p6(d):
        to, dev = zdev(d)
        return remote(att.at[0, zrows], att.at[0, zrows], s_p6.at[d], r_p6.at[d], dev)

    for d in range(1, NZ):
        copy = p6(d)
        copy.start()
        sends.append(copy)
    for d in range(1, NZ):
        p6(d).wait_recv()
    across = remote(att.at[0], att.at[1], s_rc, r_rc, twin)
    across.start()
    sends.append(across)

    for d in range(1, NY):
        out_weights(d).wait_recv()
    head_rows = pl.ds(pl.multiple_of(core * 128, 128), 128)
    twin_rows = pl.ds(pl.multiple_of(other * 128, 128), 128)
    first = [dot(att[0], wo[b, head_rows, :]) for b in range(NY)]
    across.wait_recv()
    for b in range(NY):
        o2s[b] = (first[b] + dot(att[1], wo[b, twin_rows, :])).astype(BF16)

    def p7_copy(i):
        ty, tx, th = lax.rem(y + i % 4, 4), lax.rem(x + i // 8, 4), lax.rem(h + (i // 4) % 2, 2)
        rows = pl.ds(pl.multiple_of((tx * NH + th) * 32, 32), 32)
        return remote(
            o2s.at[ty, rows], p7.at[tp * NY + y], s_p7.at[i], r_p7.at[i], device(z, ty, core, tx, th)
        )

    def p7_start(i, carry):
        p7_copy(i).start()
        return carry

    def p7_recv(i, carry):
        p7_copy(i).wait_recv()
        return carry

    def p7_send(i, carry):
        p7_copy(i).wait_send()
        return carry

    lax.fori_loop(1, 32, p7_start, 0)
    p7[tp * NY + y] = o2s[y, own_rows, :]
    lax.fori_loop(1, 32, p7_recv, 0)
    result = p7[0].astype(F32)
    for b in range(1, 32):
        result = result + p7[b].astype(F32)
    out_ref[...] = result

    for copy in sends:
        copy.wait_send()
    lax.fori_loop(1, 32, p7_send, 0)


def per_device(hidden_in, w_query, w_key, w_value, w_out, cache_keys, cache_values, prefix_lengths):
    dma = pltpu.SemaphoreType.DMA
    vmem = pltpu.VMEM
    in_hbm = pl.BlockSpec(memory_space=pltpu.HBM)
    return pl.pallas_call(
        kernel,
        out_shape=jax.ShapeDtypeStruct((32, 128), F32),
        in_specs=[in_hbm] * 7 + [pl.BlockSpec(memory_space=pltpu.SMEM)],
        out_specs=pl.BlockSpec(memory_space=pltpu.VMEM),
        scratch_shapes=[
            vmem((256, 512), BF16), vmem((128, 1024), BF16), vmem((2, 128, 128), BF16), vmem((1024, 128), BF16),
            vmem((4, 128, 256), BF16), vmem((4, 128, 128), BF16),
            vmem((4, 256, 128), BF16), vmem((8, 512, 128), BF16), vmem((8, 512, 128), BF16),
            vmem((3, 256, 128), F32), vmem((256, 128), F32), vmem((8, 8, 128), F32), vmem((8, 8, 128), F32),
            vmem((8, 40, 128), F32), vmem((8, 40, 128), F32), vmem((2, 256, 128), BF16), vmem((8, 16, 128), F32),
            vmem((512, 1), F32), vmem((512, 1), F32), vmem((512, 128), F32),
            vmem((2, 8, 48, 128), BF16), vmem((2, 8, 48, 128), BF16),
            vmem((2, 256, 128), BF16), vmem((4, 256, 128), BF16), vmem((32, 32, 128), BF16),
            dma((7,)), dma((8,)), dma((8,)), dma((4,)), dma((4,)), dma((2, 4)), dma((2, 4)), dma((4,)), dma((4,)),
            dma((2,)), dma((2,)), dma((2,)), dma((2,)), dma((2,)), dma((2,)),
            dma((2,)), dma((2,)), dma((8,)), dma((8,)), dma((2, 8)), dma((2, 8)), dma((2, 4)), dma((2, 4)),
            dma((2, 8)), dma((2, 8)), dma((8,)), dma((8,)), dma, dma, dma((32,)), dma((32,)),
        ],
        compiler_params=pltpu.CompilerParams(
            collective_id=0, has_side_effects=True, vmem_limit_bytes=56 * 1024 * 1024
        ),
        cost_estimate=pl.CostEstimate(flops=1_000_000_000, bytes_accessed=2_000_000, transcendentals=1_100_000),
        name="attention_block",
    )(
        hidden_in, w_query, w_key, w_value, w_out,
        cache_keys.reshape(cache_keys.shape[0], 128), cache_values.reshape(cache_values.shape[0], 128),
        prefix_lengths,
    )


def solution(mesh):
    placed = (
        P("tp", "ctx"),
        P("ctx", "tp"),
        P("ctx", "tp"),
        P("ctx", "tp"),
        P("tp", "ctx"),
        P("ctx", "tp", None),
        P("ctx", "tp", None),
        P("ctx"),
    )
    return jax.shard_map(
        per_device, mesh=mesh, in_specs=placed, out_specs=P("tp", "ctx"), check_vma=False
    )
```

```python
import functools
import math

import jax
import jax.numpy as jnp
from jax import lax
from jax.experimental import pallas as pl
from jax.experimental.pallas import tpu as pltpu
from jax.sharding import PartitionSpec as P

MESH = pl.DeviceIdType.MESH
F32 = jnp.float32
BF16 = jnp.bfloat16
NZ, NY, NX, NH = 8, 4, 4, 2
LOG2E = 1.0 / math.log(2.0)
NEG = -1e30
KEYS_WITH = 1
HEADS_WITH = 2
GROUPS = (
    "hidden", "query weights", "kv weights", "cache twin", "cache line", "cache relay", "out weights", "pair",
    "queries", "kv pair", "kv", "heads 0", "heads 1", "messages", "partials 0", "partials 1", "attended", "across",
    "plane",
)


def coords():
    c = lax.axis_index("ctx")
    t = lax.axis_index("tp")
    return c // 8, (c // 2) % 4, c % 2, t // 2, t % 2


def device(z, y, core, x, h):
    return ((z * NY + y) * 2 + core, x * NH + h)


def dot(a, b):
    return jnp.dot(a, b, preferred_element_type=F32)


def dot_t(a, b):
    return lax.dot_general(a, b, (((1,), (1,)), ((), ())), preferred_element_type=F32)


def kernel(
    hid_ref, wq_ref, wk_ref, wv_ref, wo_ref, ck_ref, cv_ref, len_ref, out_ref,
    hs, wqs, wkvs, wos, wq, wkv, wo, kb, vb, yp, yin, yk, kvs, kvin, p2s, p2d, p2k, p2e, qb, msgs,
    po, pod, att, o2s, p7, loc, ssem, rsem, s_hx, r_hx,
):
    z, y, core, x, h = coords()
    other = 1 - core
    yf = h * NY + y
    tp = x * NH + h
    mine = y * 2 + core
    own_rows = pl.ds(pl.multiple_of(tp * 32, 32), 32)
    own_cols = pl.ds(pl.multiple_of(y * 128, 128), 128)
    zrows = pl.ds(pl.multiple_of(z * 32, 32), 32)

    def xor_y(bits):
        if bits == 1:
            return y + 1 - 2 * (y % 2)
        return lax.rem(y + 2, NY)

    keys_y, heads_y = xor_y(KEYS_WITH), xor_y(HEADS_WITH)
    twin = device(z, y, other, x, h)

    def remote(src, dst, ssem, rsem, dev):
        return pltpu.make_async_remote_copy(
            src_ref=src, dst_ref=dst, send_sem=ssem, recv_sem=rsem, device_id=dev, device_id_type=MESH
        )

    sent = []

    def group(name, size):
        index = GROUPS.index(name)

        def put(src, dst, dev):
            remote(src, dst, ssem.at[index], rsem.at[index], dev).start()

        def arrived():
            remote(size, size, ssem.at[index], rsem.at[index], twin).wait_recv()

        sent.append(lambda: remote(size, size, ssem.at[index], rsem.at[index], twin).wait_send())
        return put, arrived

    local = [
        pltpu.make_async_copy(hid_ref, hs.at[own_rows, own_cols], loc.at[0]),
        pltpu.make_async_copy(wq_ref, wqs, loc.at[1]),
        pltpu.make_async_copy(wk_ref, wkvs.at[0], loc.at[2]),
        pltpu.make_async_copy(wv_ref, wkvs.at[1], loc.at[3]),
        pltpu.make_async_copy(ck_ref, kb.at[0], loc.at[4]),
        pltpu.make_async_copy(cv_ref, vb.at[0], loc.at[5]),
        pltpu.make_async_copy(wo_ref, wos, loc.at[6]),
    ]
    for copy in local:
        copy.start()

    barrier = pltpu.get_barrier_semaphore()

    def greet(dev):
        pl.semaphore_signal(barrier, inc=1, device_id=dev, device_id_type=MESH)

    def plane(i):
        return lax.rem(y + i % 4, 4), lax.rem(x + i // 8, 4), lax.rem(h + (i // 4) % 2, 2)

    def greet_plane(i, carry):
        to_y, to_x, to_h = plane(i)
        greet(device(z, to_y, core, to_x, to_h))
        return carry

    lax.fori_loop(1, 32, greet_plane, 0)
    for d in range(1, NZ):
        greet(device(lax.rem(z + d, NZ), y, core, x, h))
        greet(device(lax.rem(z + d, NZ), heads_y, core, x, h))
    for d in range(NY):
        greet(device(z, lax.rem(y + d, NY), other, x, h))
    pl.semaphore_wait(barrier, 31 + 2 * (NZ - 1) + NY)

    own_hidden = hs.at[own_rows, own_cols]
    put, hidden_y_arrived = group("hidden", hs.at[0:224, 0:128])
    local[0].wait()
    for d in (4, 3, 5, 2, 6, 1, 7):
        to = lax.rem(yf + d, 8)
        put(own_hidden, own_hidden, device(z, to % 4, core, x, to // 4))

    put, query_weights_arrived = group("query weights", wq.at[0:3])
    local[1].wait()
    for d in (2, 3, 1):
        to = lax.rem(y + d, NY)
        put(wqs.at[:, pl.ds(pl.multiple_of(to * 256, 256), 256)], wq.at[y], device(z, to, core, x, h))
    wq[y] = wqs[:, pl.ds(pl.multiple_of(y * 256, 256), 256)]

    put, cache_twin_arrived = group("cache twin", kb.at[0:2])
    for i, buf in enumerate((kb, vb)):
        local[4 + i].wait()
        put(buf.at[0], buf.at[1], twin)
    for copy in local[2:4]:
        copy.wait()
    wkv[y] = wkvs[y % 2]

    hidden_y_arrived()

    def hidden_x(d):
        rows = pl.ds(pl.multiple_of(x * 64, 64), 64)
        return remote(hs.at[rows], hs.at[rows], s_hx.at[d], r_hx.at[d], device(z, y, core, lax.rem(x + d, NX), h))

    for d in (2, 1, 3):
        hidden_x(d).start()

    put, kv_weights_arrived = group("kv weights", wkv.at[0:3])
    for d in (2, 3, 1):
        to = lax.rem(y + d, NY)
        put(wkvs.at[to % 2], wkv.at[y], device(z, to, core, x, h))

    query_weights_arrived()
    put, cache_line_arrived = group("cache line", kb.at[0:2])
    for buf in (kb, vb):
        put(buf.at[0], buf.at[2], device(z, keys_y, core, x, h))
    wqf = wq[...].reshape(512, 256)

    def project(block):
        rows = pl.ds(pl.multiple_of(block * 64, 64), 64)
        both = dot(hs[rows, :], wqf)
        yp[0, rows, :] = both[:, :128]
        yp[1, rows, :] = both[:, 128:]

    project(x)
    for d in (1, 3, 2):
        hidden_x(d).wait_recv()
        project(lax.rem(x + NX - d, NX))

    put, pair_arrived = group("pair", yin)
    put(yp.at[other], yin, twin)

    put, out_weights_arrived = group("out weights", wo.at[0:3])
    local[6].wait()
    for d in (2, 3, 1):
        to = lax.rem(y + d, NY)
        put(wos.at[pl.ds(pl.multiple_of(to * 256, 256), 256)], wo.at[y], device(z, to, core, x, h))
    wo[y] = wos[pl.ds(pl.multiple_of(y * 256, 256), 256), :]

    pair_arrived()
    for b in range(NZ):
        rows = slice(32 * b, 32 * b + 32)
        p2s[b] = yp[core, rows, :] + yin[rows, :]

    def zdev(d, at_y=y):
        to = lax.rem(z + d, NZ)
        return to, device(to, at_y, core, x, h)

    put, queries_arrived = group("queries", p2d.at[0:7])
    for d in (4, 3, 5, 2, 6, 1, 7):
        to, dev = zdev(d)
        put(p2s.at[to], p2d.at[z], dev)
    p2d[z] = p2s[z]

    kv_weights_arrived()
    yk[...] = dot(hs[...], wkv[...].reshape(512, 128))
    half = 16 * (y // 2)
    for b in range(NZ):
        kvs[b] = yk[pl.ds(pl.multiple_of(32 * b + half + 8 * other, 8), 8), :]
    put, kv_pair_arrived = group("kv pair", kvs)
    put(kvs, kvin, twin)
    kv_pair_arrived()
    for b in range(NZ):
        p2k[b] = yk[pl.ds(pl.multiple_of(32 * b + half + 8 * core, 8), 8), :] + kvin[b]
    put, kv_arrived = group("kv", p2e.at[0:7])
    for d in (4, 3, 5, 2, 6, 1, 7):
        to, dev = zdev(d)
        put(p2k.at[to], p2e.at[z], dev)
    p2e[z] = p2k[z]

    queries_arrived()
    total = p2d[0]
    for b in range(1, NZ):
        total = total + p2d[b]
    qb[0, zrows, :] = total.astype(BF16)
    put0, heads0_arrived = group("heads 0", qb.at[0, 0:224])
    put1, heads1_arrived = group("heads 1", qb.at[1])
    for d in (4, 3, 5, 2, 6, 1, 7, 0):
        put1(qb.at[0, zrows], qb.at[1, zrows], zdev(d, heads_y)[1])
    for d in (4, 3, 5, 2, 6, 1, 7):
        put0(qb.at[0, zrows], qb.at[0, zrows], zdev(d)[1])

    kv_arrived()
    total = p2e[0]
    for b in range(1, NZ):
        total = total + p2e[b]
    msgs[mine, 0:8, :] = total
    msgs[mine, 8:16, :] = jnp.full((8, 128), len_ref[0].astype(F32), F32)
    put, messages_arrived = group("messages", msgs.at[0:7])
    for d in (2, 3, 1, 0):
        for k in range(2):
            if (d, k) != (0, 0):
                put(msgs.at[mine], msgs.at[mine], device(z, lax.rem(y + d, NY), lax.rem(core + k, 2), x, h))

    cache_line_arrived()
    put, cache_relay_arrived = group("cache relay", kb.at[0:2])
    for buf in (kb, vb):
        put(buf.at[2], buf.at[3], twin)
    cache_twin_arrived()
    messages_arrived()
    cache_relay_arrived()

    scale = LOG2E / math.sqrt(128.0)
    place = lax.broadcasted_iota(jnp.int32, (1, 512), 1).astype(F32)
    bias = []
    for index in (mine, y * 2 + other, keys_y * 2 + core, keys_y * 2 + other):
        filled = jnp.concatenate([msgs[index, 8:9, :]] * 4, axis=1)
        bias.append(jnp.where(place < filled, 0.0, NEG))
    bias = jnp.concatenate(bias, axis=1)
    keys = kb[...].reshape(2048, 128)
    values = vb[...].reshape(2048, 128)
    diagonal = lax.broadcasted_iota(jnp.int32, (32, 128), 0) == lax.broadcasted_iota(jnp.int32, (32, 128), 1)
    row16 = lax.broadcasted_iota(jnp.int32, (16, 128), 0)

    def attend(j, new):
        queries = qb[j]
        scores = dot_t(queries, keys) * scale + bias
        top = jnp.max(scores, axis=1, keepdims=True)
        if new:
            new_keys = jnp.concatenate([msgs[i, 0:8, :] for i in (0, 1, 4, 5)], axis=0).astype(BF16)
            new_values = jnp.concatenate([msgs[i, 0:8, :] for i in (2, 3, 6, 7)], axis=0).astype(BF16)
            key_at = lax.broadcasted_iota(jnp.int32, (256, 32), 1) + z * 32
            row_at = lax.broadcasted_iota(jnp.int32, (256, 32), 0)
            fresh = jnp.where(key_at <= row_at, dot_t(queries, new_keys) * scale, NEG)
            top = jnp.maximum(top, jnp.max(fresh, axis=1, keepdims=True))
        weight = jnp.exp2(scores - top)
        sums = jnp.sum(weight, axis=1, keepdims=True)
        mixed = dot(weight.astype(BF16), values)
        if new:
            weight = jnp.exp2(fresh - top)
            sums = sums + jnp.sum(weight, axis=1, keepdims=True)
            mixed = mixed + dot(weight.astype(BF16), new_values)
        shared = (mixed / sums).astype(BF16)
        level = top + jnp.log2(sums)
        for b in range(NZ):
            rows = slice(32 * b, 32 * b + 32)
            po[j, b, 0:32, :] = shared[rows]
            line = jnp.sum(jnp.where(diagonal, level[rows], 0.0), axis=0, keepdims=True)
            high = line.astype(BF16).astype(F32)
            mid = (line - high).astype(BF16).astype(F32)
            low = line - high - mid
            po[j, b, 32:48, :] = jnp.where(row16 == 0, high, jnp.where(row16 == 1, mid, low)).astype(BF16)

    put0, partials0_arrived = group("partials 0", pod.at[0, 0:7])
    put1, partials1_arrived = group("partials 1", pod.at[1])
    heads1_arrived()
    attend(1, False)
    for d in (4, 3, 5, 2, 6, 1, 7, 0):
        to, dev = zdev(d, heads_y)
        put1(po.at[1, to], pod.at[1, z], dev)
    heads0_arrived()
    attend(0, True)
    for d in (4, 3, 5, 2, 6, 1, 7):
        to, dev = zdev(d)
        put0(po.at[0, to], pod.at[0, z], dev)
    pod[0, z] = po[0, z]
    partials0_arrived()
    partials1_arrived()

    levels, parts = [], []
    for j in range(2):
        for b in range(NZ):
            rows = pod[j, b, 32:48, :].astype(F32)
            line = rows[0:1] + rows[1:2] + rows[2:3]
            spread = jnp.where(diagonal, jnp.broadcast_to(line, (32, 128)), 0.0)
            levels.append(jnp.sum(spread, axis=1, keepdims=True))
            parts.append(pod[j, b, 0:32, :].astype(F32))
    top = functools.reduce(jnp.maximum, levels)
    shares = [jnp.exp2(one - top) for one in levels]
    whole = functools.reduce(jnp.add, shares)
    merged = functools.reduce(jnp.add, [part * share for part, share in zip(parts, shares)])
    att[0, zrows, :] = (merged / whole).astype(BF16)

    put, attended_arrived = group("attended", att.at[0, 0:224])
    for d in (4, 3, 5, 2, 6, 1, 7):
        put(att.at[0, zrows], att.at[0, zrows], zdev(d)[1])
    out_weights_arrived()
    attended_arrived()
    put, across_arrived = group("across", att.at[1])
    put(att.at[0], att.at[1], twin)

    head_rows = pl.ds(pl.multiple_of(core * 128, 128), 128)
    twin_rows = pl.ds(pl.multiple_of(other * 128, 128), 128)
    columns = [lax.rem(y + d, NY) for d in range(NY)]
    first = [dot(att[0], wo[b, head_rows, :]) for b in columns]
    across_arrived()
    put, plane_arrived = group("plane", p7.at[0:31])
    for d in range(NY):
        to_y = columns[d]
        o2s[to_y] = (first[d] + dot(att[1], wo[to_y, twin_rows, :])).astype(BF16)
        for dh in (1, 0):
            for dx in (2, 1, 3, 0):
                if (d, dh, dx) == (0, 0, 0):
                    continue
                to_x, to_h = lax.rem(x + dx, NX), lax.rem(h + dh, NH)
                rows = pl.ds(pl.multiple_of((to_x * NH + to_h) * 32, 32), 32)
                put(o2s.at[to_y, rows], p7.at[tp * NY + y], device(z, to_y, core, to_x, to_h))
    p7[tp * NY + y] = o2s[y, own_rows, :]
    for d in range(1, NX):
        hidden_x(d).wait_send()
    for wait in sent[:-1]:
        wait()
    plane_arrived()
    result = p7[0].astype(F32)
    for b in range(1, 32):
        result = result + p7[b].astype(F32)
    out_ref[...] = result
    sent[-1]()


def per_device(hidden_in, w_query, w_key, w_value, w_out, cache_keys, cache_values, prefix_lengths):
    dma = pltpu.SemaphoreType.DMA
    vmem = pltpu.VMEM
    in_hbm = pl.BlockSpec(memory_space=pltpu.HBM)
    return pl.pallas_call(
        kernel,
        out_shape=jax.ShapeDtypeStruct((32, 128), F32),
        in_specs=[in_hbm] * 7 + [pl.BlockSpec(memory_space=pltpu.SMEM)],
        out_specs=pl.BlockSpec(memory_space=pltpu.VMEM),
        scratch_shapes=[
            vmem((256, 512), BF16), vmem((128, 1024), BF16), vmem((2, 128, 128), BF16), vmem((1024, 128), BF16),
            vmem((4, 128, 256), BF16), vmem((4, 128, 128), BF16), vmem((4, 256, 128), BF16),
            vmem((4, 512, 128), BF16), vmem((4, 512, 128), BF16),
            vmem((2, 256, 128), F32), vmem((256, 128), F32), vmem((256, 128), F32),
            vmem((8, 8, 128), F32), vmem((8, 8, 128), F32),
            vmem((8, 32, 128), F32), vmem((8, 32, 128), F32), vmem((8, 8, 128), F32), vmem((8, 8, 128), F32),
            vmem((2, 256, 128), BF16), vmem((8, 16, 128), F32),
            vmem((2, 8, 48, 128), BF16), vmem((2, 8, 48, 128), BF16),
            vmem((2, 256, 128), BF16), vmem((4, 256, 128), BF16), vmem((32, 32, 128), BF16),
            dma((7,)), dma((len(GROUPS),)), dma((len(GROUPS),)), dma((4,)), dma((4,)),
        ],
        compiler_params=pltpu.CompilerParams(
            collective_id=0, has_side_effects=True, vmem_limit_bytes=56 * 1024 * 1024
        ),
        cost_estimate=pl.CostEstimate(flops=1_000_000_000, bytes_accessed=2_000_000, transcendentals=1_100_000),
        name="attention_block",
    )(
        hidden_in, w_query, w_key, w_value, w_out,
        cache_keys.reshape(cache_keys.shape[0], 128), cache_values.reshape(cache_values.shape[0], 128),
        prefix_lengths,
    )


def solution(mesh):
    placed = (
        P("tp", "ctx"),
        P("ctx", "tp"),
        P("ctx", "tp"),
        P("ctx", "tp"),
        P("tp", "ctx"),
        P("ctx", "tp", None),
        P("ctx", "tp", None),
        P("ctx"),
    )
    return jax.shard_map(
        per_device, mesh=mesh, in_specs=placed, out_specs=P("tp", "ctx"), check_vma=False
    )
```

```python
import functools
import math

import jax
import jax.numpy as jnp
from jax import lax
from jax.experimental import pallas as pl
from jax.experimental.pallas import tpu as pltpu
from jax.sharding import PartitionSpec as P

MESH = pl.DeviceIdType.MESH
F32 = jnp.float32
BF16 = jnp.bfloat16
NZ, NY, NX, NH = 8, 4, 4, 2
LOG2E = 1.0 / math.log(2.0)
NEG = -1e30
KEYS_WITH = 1
HEADS_WITH = 2
GROUPS = (
    "hidden", "query weights", "kv weights", "cache twin", "cache line", "cache relay", "out weights", "pair",
    "queries", "kv pair", "kv", "heads 0", "heads 1", "messages", "partials 0", "partials 1", "attended", "across",
    "plane",
)


def coords():
    c = lax.axis_index("ctx")
    t = lax.axis_index("tp")
    return c // 8, (c // 2) % 4, c % 2, t // 2, t % 2


def device(z, y, core, x, h):
    return ((z * NY + y) * 2 + core, x * NH + h)


def dot(a, b):
    return jnp.dot(a, b, preferred_element_type=F32)


def dot_t(a, b):
    return lax.dot_general(a, b, (((1,), (1,)), ((), ())), preferred_element_type=F32)


def kernel(
    hid_ref, wq_ref, wk_ref, wv_ref, wo_ref, ck_ref, cv_ref, len_ref, out_ref,
    hs, wqs, wkvs, wos, wq, wkv, wo, kb, vb, yp, yin, yk, kvs, kvin, p2s, p2d, p2k, p2e, qb, msgs,
    po, pod, att, o2s, p7, loc, ssem, rsem, s_hx, r_hx, known,
):
    z, y, core, x, h = coords()
    other = 1 - core
    yf = h * NY + y
    tp = x * NH + h
    mine = y * 2 + core
    own_rows = pl.ds(pl.multiple_of(tp * 32, 32), 32)
    own_cols = pl.ds(pl.multiple_of(y * 128, 128), 128)
    zrows = pl.ds(pl.multiple_of(z * 32, 32), 32)

    def xor_y(bits):
        if bits == 1:
            return y + 1 - 2 * (y % 2)
        return lax.rem(y + 2, NY)

    keys_y, heads_y = xor_y(KEYS_WITH), xor_y(HEADS_WITH)
    twin = device(z, y, other, x, h)

    def remote(src, dst, ssem, rsem, dev):
        return pltpu.make_async_remote_copy(
            src_ref=src, dst_ref=dst, send_sem=ssem, recv_sem=rsem, device_id=dev, device_id_type=MESH
        )

    sent = []

    def group(name, size):
        index = GROUPS.index(name)

        def put(src, dst, dev):
            remote(src, dst, ssem.at[index], rsem.at[index], dev).start()

        def arrived():
            remote(size, size, ssem.at[index], rsem.at[index], twin).wait_recv()

        sent.append(lambda: remote(size, size, ssem.at[index], rsem.at[index], twin).wait_send())
        return put, arrived

    local = [
        pltpu.make_async_copy(hid_ref, hs.at[own_rows, own_cols], loc.at[0]),
        pltpu.make_async_copy(wq_ref, wqs, loc.at[1]),
        pltpu.make_async_copy(wk_ref, wkvs.at[0], loc.at[2]),
        pltpu.make_async_copy(wv_ref, wkvs.at[1], loc.at[3]),
        pltpu.make_async_copy(ck_ref, kb.at[0], loc.at[4]),
        pltpu.make_async_copy(cv_ref, vb.at[0], loc.at[5]),
        pltpu.make_async_copy(wo_ref, wos, loc.at[6]),
    ]
    for copy in local:
        copy.start()

    barrier = pltpu.get_barrier_semaphore()

    def zdev(d, at_y=y):
        to = lax.rem(z + d, NZ)
        return to, device(to, at_y, core, x, h)

    def yring(d):
        to = lax.rem(yf + d, 8)
        return device(z, to % 4, core, x, to // 4)

    near = [yring(d) for d in (4, 3, 5, 2, 6, 1, 7)]
    near += [device(z, y, core, lax.rem(x + d, NX), h) for d in (2, 1, 3)]
    near += [zdev(1)[1], zdev(7)[1], twin]
    for dev in near:
        pl.semaphore_signal(barrier, inc=1, device_id=dev, device_id_type=MESH)
    pl.semaphore_wait(barrier, len(near))

    def tell(i, d):
        pl.semaphore_signal(known.at[i], inc=1, device_id=zdev(d)[1], device_id_type=MESH)

    own_hidden = hs.at[own_rows, own_cols]
    put, hidden_y_arrived = group("hidden", hs.at[0:224, 0:128])
    local[0].wait()
    for d in (4, 3, 5, 2, 6, 1, 7):
        put(own_hidden, own_hidden, yring(d))
    tell(0, 1)
    tell(1, 7)

    put, query_weights_arrived = group("query weights", wq.at[0:3])
    local[1].wait()
    for d in (2, 3, 1):
        to = lax.rem(y + d, NY)
        put(wqs.at[:, pl.ds(pl.multiple_of(to * 256, 256), 256)], wq.at[y], device(z, to, core, x, h))
    wq[y] = wqs[:, pl.ds(pl.multiple_of(y * 256, 256), 256)]

    put, cache_twin_arrived = group("cache twin", kb.at[0:2])
    for i, buf in enumerate((kb, vb)):
        local[4 + i].wait()
        put(buf.at[0], buf.at[1], twin)
    for copy in local[2:4]:
        copy.wait()
    wkv[y] = wkvs[y % 2]

    for i in range(2):
        pl.semaphore_wait(known.at[i], 1)
    tell(2, 1)
    tell(3, 7)
    tell(4, 2)
    hidden_y_arrived()

    def hidden_x(d):
        rows = pl.ds(pl.multiple_of(x * 64, 64), 64)
        return remote(hs.at[rows], hs.at[rows], s_hx.at[d], r_hx.at[d], device(z, y, core, lax.rem(x + d, NX), h))

    for d in (2, 1, 3):
        hidden_x(d).start()

    put, kv_weights_arrived = group("kv weights", wkv.at[0:3])
    for d in (2, 3, 1):
        to = lax.rem(y + d, NY)
        put(wkvs.at[to % 2], wkv.at[y], device(z, to, core, x, h))

    query_weights_arrived()
    put, cache_line_arrived = group("cache line", kb.at[0:2])
    for buf in (kb, vb):
        put(buf.at[0], buf.at[2], device(z, keys_y, core, x, h))
    wqf = wq[...].reshape(512, 256)

    def project(block):
        rows = pl.ds(pl.multiple_of(block * 64, 64), 64)
        both = dot(hs[rows, :], wqf)
        yp[0, rows, :] = both[:, :128]
        yp[1, rows, :] = both[:, 128:]

    project(x)
    for d in (1, 3, 2):
        hidden_x(d).wait_recv()
        project(lax.rem(x + NX - d, NX))

    put, pair_arrived = group("pair", yin)
    put(yp.at[other], yin, twin)

    put, out_weights_arrived = group("out weights", wo.at[0:3])
    local[6].wait()
    for d in (2, 3, 1):
        to = lax.rem(y + d, NY)
        put(wos.at[pl.ds(pl.multiple_of(to * 256, 256), 256)], wo.at[y], device(z, to, core, x, h))
    wo[y] = wos[pl.ds(pl.multiple_of(y * 256, 256), 256), :]

    pair_arrived()
    for b in range(NZ):
        rows = slice(32 * b, 32 * b + 32)
        p2s[b] = yp[core, rows, :] + yin[rows, :]

    for i in range(2, 5):
        pl.semaphore_wait(known.at[i], 1)
    put, queries_arrived = group("queries", p2d.at[0:7])
    for d in (4, 3, 5, 2, 6, 1, 7):
        to, dev = zdev(d)
        put(p2s.at[to], p2d.at[z], dev)
    p2d[z] = p2s[z]

    kv_weights_arrived()
    yk[...] = dot(hs[...], wkv[...].reshape(512, 128))
    half = 16 * (y // 2)
    for b in range(NZ):
        kvs[b] = yk[pl.ds(pl.multiple_of(32 * b + half + 8 * other, 8), 8), :]
    put, kv_pair_arrived = group("kv pair", kvs)
    put(kvs, kvin, twin)
    kv_pair_arrived()
    for b in range(NZ):
        p2k[b] = yk[pl.ds(pl.multiple_of(32 * b + half + 8 * core, 8), 8), :] + kvin[b]
    put, kv_arrived = group("kv", p2e.at[0:7])
    for d in (4, 3, 5, 2, 6, 1, 7):
        to, dev = zdev(d)
        put(p2k.at[to], p2e.at[z], dev)
    p2e[z] = p2k[z]

    queries_arrived()
    total = p2d[0]
    for b in range(1, NZ):
        total = total + p2d[b]
    qb[0, zrows, :] = total.astype(BF16)
    put0, heads0_arrived = group("heads 0", qb.at[0, 0:224])
    put1, heads1_arrived = group("heads 1", qb.at[1])
    for d in (4, 3, 5, 2, 6, 1, 7, 0):
        put1(qb.at[0, zrows], qb.at[1, zrows], zdev(d, heads_y)[1])
    for d in (4, 3, 5, 2, 6, 1, 7):
        put0(qb.at[0, zrows], qb.at[0, zrows], zdev(d)[1])

    kv_arrived()
    total = p2e[0]
    for b in range(1, NZ):
        total = total + p2e[b]
    msgs[mine, 0:8, :] = total
    msgs[mine, 8:16, :] = jnp.full((8, 128), len_ref[0].astype(F32), F32)
    put, messages_arrived = group("messages", msgs.at[0:7])
    for d in (2, 3, 1, 0):
        for k in range(2):
            if (d, k) != (0, 0):
                put(msgs.at[mine], msgs.at[mine], device(z, lax.rem(y + d, NY), lax.rem(core + k, 2), x, h))

    cache_line_arrived()
    put, cache_relay_arrived = group("cache relay", kb.at[0:2])
    for buf in (kb, vb):
        put(buf.at[2], buf.at[3], twin)
    cache_twin_arrived()
    messages_arrived()
    cache_relay_arrived()

    scale = LOG2E / math.sqrt(128.0)
    place = lax.broadcasted_iota(jnp.int32, (1, 512), 1).astype(F32)
    bias = []
    for index in (mine, y * 2 + other, keys_y * 2 + core, keys_y * 2 + other):
        filled = jnp.concatenate([msgs[index, 8:9, :]] * 4, axis=1)
        bias.append(jnp.where(place < filled, 0.0, NEG))
    bias = jnp.concatenate(bias, axis=1)
    keys = kb[...].reshape(2048, 128)
    values = vb[...].reshape(2048, 128)
    diagonal = lax.broadcasted_iota(jnp.int32, (32, 128), 0) == lax.broadcasted_iota(jnp.int32, (32, 128), 1)
    row16 = lax.broadcasted_iota(jnp.int32, (16, 128), 0)

    def attend(j, new):
        queries = qb[j]
        scores = dot_t(queries, keys) * scale + bias
        top = jnp.max(scores, axis=1, keepdims=True)
        if new:
            new_keys = jnp.concatenate([msgs[i, 0:8, :] for i in (0, 1, 4, 5)], axis=0).astype(BF16)
            new_values = jnp.concatenate([msgs[i, 0:8, :] for i in (2, 3, 6, 7)], axis=0).astype(BF16)
            key_at = lax.broadcasted_iota(jnp.int32, (256, 32), 1) + z * 32
            row_at = lax.broadcasted_iota(jnp.int32, (256, 32), 0)
            fresh = jnp.where(key_at <= row_at, dot_t(queries, new_keys) * scale, NEG)
            top = jnp.maximum(top, jnp.max(fresh, axis=1, keepdims=True))
        weight = jnp.exp2(scores - top)
        sums = jnp.sum(weight, axis=1, keepdims=True)
        mixed = dot(weight.astype(BF16), values)
        if new:
            weight = jnp.exp2(fresh - top)
            sums = sums + jnp.sum(weight, axis=1, keepdims=True)
            mixed = mixed + dot(weight.astype(BF16), new_values)
        shared = (mixed / sums).astype(BF16)
        level = top + jnp.log2(sums)
        for b in range(NZ):
            rows = slice(32 * b, 32 * b + 32)
            po[j, b, 0:32, :] = shared[rows]
            line = jnp.sum(jnp.where(diagonal, level[rows], 0.0), axis=0, keepdims=True)
            high = line.astype(BF16).astype(F32)
            mid = (line - high).astype(BF16).astype(F32)
            low = line - high - mid
            po[j, b, 32:48, :] = jnp.where(row16 == 0, high, jnp.where(row16 == 1, mid, low)).astype(BF16)

    put0, partials0_arrived = group("partials 0", pod.at[0, 0:7])
    put1, partials1_arrived = group("partials 1", pod.at[1])
    heads1_arrived()
    attend(1, False)
    for d in (4, 3, 5, 2, 6, 1, 7, 0):
        to, dev = zdev(d, heads_y)
        put1(po.at[1, to], pod.at[1, z], dev)
    heads0_arrived()
    attend(0, True)
    for d in (4, 3, 5, 2, 6, 1, 7):
        to, dev = zdev(d)
        put0(po.at[0, to], pod.at[0, z], dev)
    pod[0, z] = po[0, z]
    partials0_arrived()
    partials1_arrived()

    levels, parts = [], []
    for j in range(2):
        for b in range(NZ):
            rows = pod[j, b, 32:48, :].astype(F32)
            line = rows[0:1] + rows[1:2] + rows[2:3]
            spread = jnp.where(diagonal, jnp.broadcast_to(line, (32, 128)), 0.0)
            levels.append(jnp.sum(spread, axis=1, keepdims=True))
            parts.append(pod[j, b, 0:32, :].astype(F32))
    top = functools.reduce(jnp.maximum, levels)
    shares = [jnp.exp2(one - top) for one in levels]
    whole = functools.reduce(jnp.add, shares)
    merged = functools.reduce(jnp.add, [part * share for part, share in zip(parts, shares)])
    att[0, zrows, :] = (merged / whole).astype(BF16)

    put, attended_arrived = group("attended", att.at[0, 0:224])
    for d in (4, 3, 5, 2, 6, 1, 7):
        put(att.at[0, zrows], att.at[0, zrows], zdev(d)[1])
    out_weights_arrived()
    attended_arrived()
    put, across_arrived = group("across", att.at[1])
    put(att.at[0], att.at[1], twin)

    head_rows = pl.ds(pl.multiple_of(core * 128, 128), 128)
    twin_rows = pl.ds(pl.multiple_of(other * 128, 128), 128)
    columns = [lax.rem(y + d, NY) for d in range(NY)]
    first = [dot(att[0], wo[b, head_rows, :]) for b in columns]
    across_arrived()
    put, plane_arrived = group("plane", p7.at[0:31])
    for d in range(NY):
        to_y = columns[d]
        o2s[to_y] = (first[d] + dot(att[1], wo[to_y, twin_rows, :])).astype(BF16)
        for dh in (1, 0):
            for dx in (2, 1, 3, 0):
                if (d, dh, dx) == (0, 0, 0):
                    continue
                to_x, to_h = lax.rem(x + dx, NX), lax.rem(h + dh, NH)
                rows = pl.ds(pl.multiple_of((to_x * NH + to_h) * 32, 32), 32)
                put(o2s.at[to_y, rows], p7.at[tp * NY + y], device(z, to_y, core, to_x, to_h))
    p7[tp * NY + y] = o2s[y, own_rows, :]
    for d in range(1, NX):
        hidden_x(d).wait_send()
    for wait in sent[:-1]:
        wait()
    plane_arrived()
    result = p7[0].astype(F32)
    for b in range(1, 32):
        result = result + p7[b].astype(F32)
    out_ref[...] = result
    sent[-1]()


def per_device(hidden_in, w_query, w_key, w_value, w_out, cache_keys, cache_values, prefix_lengths):
    dma = pltpu.SemaphoreType.DMA
    vmem = pltpu.VMEM
    in_hbm = pl.BlockSpec(memory_space=pltpu.HBM)
    return pl.pallas_call(
        kernel,
        out_shape=jax.ShapeDtypeStruct((32, 128), F32),
        in_specs=[in_hbm] * 7 + [pl.BlockSpec(memory_space=pltpu.SMEM)],
        out_specs=pl.BlockSpec(memory_space=pltpu.VMEM),
        scratch_shapes=[
            vmem((256, 512), BF16), vmem((128, 1024), BF16), vmem((2, 128, 128), BF16), vmem((1024, 128), BF16),
            vmem((4, 128, 256), BF16), vmem((4, 128, 128), BF16), vmem((4, 256, 128), BF16),
            vmem((4, 512, 128), BF16), vmem((4, 512, 128), BF16),
            vmem((2, 256, 128), F32), vmem((256, 128), F32), vmem((256, 128), F32),
            vmem((8, 8, 128), F32), vmem((8, 8, 128), F32),
            vmem((8, 32, 128), F32), vmem((8, 32, 128), F32), vmem((8, 8, 128), F32), vmem((8, 8, 128), F32),
            vmem((2, 256, 128), BF16), vmem((8, 16, 128), F32),
            vmem((2, 8, 48, 128), BF16), vmem((2, 8, 48, 128), BF16),
            vmem((2, 256, 128), BF16), vmem((4, 256, 128), BF16), vmem((32, 32, 128), BF16),
            dma((7,)), dma((len(GROUPS),)), dma((len(GROUPS),)), dma((4,)), dma((4,)),
            pltpu.SemaphoreType.REGULAR((5,)),
        ],
        compiler_params=pltpu.CompilerParams(
            collective_id=0, has_side_effects=True, vmem_limit_bytes=56 * 1024 * 1024
        ),
        cost_estimate=pl.CostEstimate(flops=1_000_000_000, bytes_accessed=2_000_000, transcendentals=1_100_000),
        name="attention_block",
    )(
        hidden_in, w_query, w_key, w_value, w_out,
        cache_keys.reshape(cache_keys.shape[0], 128), cache_values.reshape(cache_values.shape[0], 128),
        prefix_lengths,
    )


def solution(mesh):
    placed = (
        P("tp", "ctx"),
        P("ctx", "tp"),
        P("ctx", "tp"),
        P("ctx", "tp"),
        P("tp", "ctx"),
        P("ctx", "tp", None),
        P("ctx", "tp", None),
        P("ctx"),
    )
    return jax.shard_map(
        per_device, mesh=mesh, in_specs=placed, out_specs=P("tp", "ctx"), check_vma=False
    )
```

```python
import functools
import math

import jax
import jax.numpy as jnp
from jax import lax
from jax.experimental import pallas as pl
from jax.experimental.pallas import tpu as pltpu
from jax.sharding import PartitionSpec as P

MESH = pl.DeviceIdType.MESH
F32 = jnp.float32
BF16 = jnp.bfloat16
NZ, NY, NX, NH = 8, 4, 4, 2
LOG2E = 1.0 / math.log(2.0)
NEG = -1e30
KEYS_WITH = 1
HEADS_WITH = 2
GROUPS = (
    "query weights", "kv weights", "cache twin", "cache line", "cache relay", "out weights", "pair",
    "queries", "kv pair", "kv", "heads 0", "heads 1", "messages", "partials 0", "partials 1", "attended", "across",
    "plane",
)


def coords():
    c = lax.axis_index("ctx")
    t = lax.axis_index("tp")
    return c // 8, (c // 2) % 4, c % 2, t // 2, t % 2


def device(z, y, core, x, h):
    return ((z * NY + y) * 2 + core, x * NH + h)


def dot(a, b):
    return jnp.dot(a, b, preferred_element_type=F32)


def dot_t(a, b):
    return lax.dot_general(a, b, (((1,), (1,)), ((), ())), preferred_element_type=F32)


def kernel(
    hid_ref, wq_ref, wk_ref, wv_ref, wo_ref, ck_ref, cv_ref, len_ref, out_ref,
    hs, wqs, wkvs, wos, wq, wkv, wo, kb, vb, yp, yin, yk, kvs, kvin, p2s, p2d, p2k, p2e, qb, msgs,
    po, pod, att, o2s, p7, loc, ssem, rsem, s_hy, r_hy, s_hx, r_hx, known,
):
    z, y, core, x, h = coords()
    other = 1 - core
    yf = h * NY + y
    tp = x * NH + h
    own_rows = pl.ds(pl.multiple_of(tp * 32, 32), 32)
    own_cols = pl.ds(pl.multiple_of(y * 128, 128), 128)
    zrows = pl.ds(pl.multiple_of(z * 32, 32), 32)

    def xor_y(bits):
        if bits == 1:
            return y + 1 - 2 * (y % 2)
        return lax.rem(y + 2, NY)

    keys_y, heads_y = xor_y(KEYS_WITH), xor_y(HEADS_WITH)
    twin = device(z, y, other, x, h)

    def remote(src, dst, ssem, rsem, dev):
        return pltpu.make_async_remote_copy(
            src_ref=src, dst_ref=dst, send_sem=ssem, recv_sem=rsem, device_id=dev, device_id_type=MESH
        )

    sent = []

    def group(name, size):
        index = GROUPS.index(name)

        def put(src, dst, dev):
            remote(src, dst, ssem.at[index], rsem.at[index], dev).start()

        def arrived():
            remote(size, size, ssem.at[index], rsem.at[index], twin).wait_recv()

        sent.append(lambda: remote(size, size, ssem.at[index], rsem.at[index], twin).wait_send())
        return put, arrived

    local = [
        pltpu.make_async_copy(hid_ref, hs.at[own_rows, own_cols], loc.at[0]),
        pltpu.make_async_copy(wq_ref, wqs, loc.at[1]),
        pltpu.make_async_copy(wk_ref, wkvs.at[0], loc.at[2]),
        pltpu.make_async_copy(wv_ref, wkvs.at[1], loc.at[3]),
        pltpu.make_async_copy(ck_ref, kb.at[0], loc.at[4]),
        pltpu.make_async_copy(cv_ref, vb.at[0], loc.at[5]),
        pltpu.make_async_copy(wo_ref, wos, loc.at[6]),
    ]
    for copy in local:
        copy.start()

    barrier = pltpu.get_barrier_semaphore()

    def zdev(d, at_y=y):
        to = lax.rem(z + d, NZ)
        return to, device(to, at_y, core, x, h)

    def yring(d):
        to = lax.rem(yf + d, 8)
        return device(z, to % 4, core, x, to // 4)

    near = [yring(d) for d in (4, 3, 5, 2, 6, 1, 7)]
    near += [device(z, y, core, lax.rem(x + d, NX), h) for d in (2, 1, 3)]
    near += [zdev(1)[1], zdev(7)[1], twin]
    for dev in near:
        pl.semaphore_signal(barrier, inc=1, device_id=dev, device_id_type=MESH)
    pl.semaphore_wait(barrier, len(near))

    def tell(i, d):
        pl.semaphore_signal(known.at[i], inc=1, device_id=zdev(d)[1], device_id_type=MESH)

    def block(d):
        at = lax.rem(yf + 8 - d, 8)
        rows = pl.ds(pl.multiple_of((x * NH + at // 4) * 32, 32), 32)
        return hs.at[rows, pl.ds(pl.multiple_of((at % 4) * 128, 128), 128)]

    def hidden_y(d):
        return remote(block(0), block(0), s_hy.at[d], r_hy.at[d], yring(d))

    def hidden_x(d, view):
        return remote(view, view, s_hx.at[d], r_hx.at[d], device(z, y, core, lax.rem(x + d, NX), h))

    def forward(d):
        for dx in (2, 1, 3):
            hidden_x(dx, block(d)).start()

    x_rows = hs.at[pl.ds(pl.multiple_of(x * 64, 64), 64)]
    local[0].wait()
    for d in (4, 3, 5, 2, 6, 1, 7):
        hidden_y(d).start()
    forward(0)
    tell(0, 1)
    tell(1, 7)

    put, query_weights_arrived = group("query weights", wq.at[0:3])
    local[1].wait()
    for d in (2, 3, 1):
        to = lax.rem(y + d, NY)
        put(wqs.at[:, pl.ds(pl.multiple_of(to * 256, 256), 256)], wq.at[y], device(z, to, core, x, h))
    wq[y] = wqs[:, pl.ds(pl.multiple_of(y * 256, 256), 256)]

    put, cache_twin_arrived = group("cache twin", kb.at[0:2])
    for i, buf in enumerate((kb, vb)):
        local[4 + i].wait()
        put(buf.at[0], buf.at[1], twin)
    for copy in local[2:4]:
        copy.wait()
    wkv[y] = wkvs[y % 2]

    for d in (1, 7, 2, 6):
        hidden_y(d).wait_recv()
        forward(d)
    for i in range(2):
        pl.semaphore_wait(known.at[i], 1)
    tell(2, 1)
    tell(3, 7)
    tell(4, 2)
    for d in (3, 5, 4):
        hidden_y(d).wait_recv()
        forward(d)

    put, kv_weights_arrived = group("kv weights", wkv.at[0:3])
    for d in (2, 3, 1):
        to = lax.rem(y + d, NY)
        put(wkvs.at[to % 2], wkv.at[y], device(z, to, core, x, h))

    query_weights_arrived()
    put, cache_line_arrived = group("cache line", kb.at[0:2])
    for buf in (kb, vb):
        put(buf.at[0], buf.at[2], device(z, keys_y, core, x, h))
    wqf = wq[...].reshape(512, 256)

    def project(block):
        rows = pl.ds(pl.multiple_of(block * 64, 64), 64)
        both = dot(hs[rows, :], wqf)
        yp[0, rows, :] = both[:, :128]
        yp[1, rows, :] = both[:, 128:]

    project(x)
    for d in (1, 3, 2):
        hidden_x(d, x_rows).wait_recv()
        project(lax.rem(x + NX - d, NX))

    put, pair_arrived = group("pair", yin)
    put(yp.at[other], yin, twin)

    put, out_weights_arrived = group("out weights", wo.at[0])
    local[6].wait()
    for pair_core in range(2):
        for chip in range(2):
            def rows_of(at):
                return pl.ds(pl.multiple_of((at // 2) * 512 + 256 * chip + 128 * pair_core, 128), 128)

            there = wo.at[pair_core, pl.ds(128 * chip, 128)]
            put(wos.at[rows_of(heads_y)], there.at[:, pl.ds(128, 128)], device(z, heads_y, core, x, h))
            wo[pair_core, 128 * chip : 128 * chip + 128, 0:128] = wos[rows_of(y), :]

    pair_arrived()
    for b in range(NZ):
        rows = slice(32 * b, 32 * b + 32)
        p2s[b] = yp[core, rows, :] + yin[rows, :]

    for i in range(2, 5):
        pl.semaphore_wait(known.at[i], 1)
    put, queries_arrived = group("queries", p2d.at[0:7])
    for d in (4, 3, 5, 2, 6, 1, 7):
        to, dev = zdev(d)
        put(p2s.at[to], p2d.at[z], dev)
    p2d[z] = p2s[z]

    kv_weights_arrived()
    yk[...] = dot(hs[...], wkv[...].reshape(512, 128))
    half = 16 * (y // 2)
    for b in range(NZ):
        p2k[b] = yk[pl.ds(pl.multiple_of(32 * b + half, 16), 16), :]
    put, kv_arrived = group("kv", p2e.at[0:7])
    for d in (4, 3, 5, 2, 6, 1, 7):
        to, dev = zdev(d)
        put(p2k.at[to], p2e.at[z], dev)
    p2e[z] = p2k[z]

    queries_arrived()
    total = p2d[0]
    for b in range(1, NZ):
        total = total + p2d[b]
    qb[0, zrows, :] = total.astype(BF16)
    put0, heads0_arrived = group("heads 0", qb.at[0, 0:224])
    put1, heads1_arrived = group("heads 1", qb.at[1])
    for d in (4, 3, 5, 2, 6, 1, 7, 0):
        put1(qb.at[0, zrows], qb.at[1, zrows], zdev(d, heads_y)[1])
    for d in (4, 3, 5, 2, 6, 1, 7):
        put0(qb.at[0, zrows], qb.at[0, zrows], zdev(d)[1])

    kv_arrived()
    total = p2e[0]
    for b in range(1, NZ):
        total = total + p2e[b]
    fill = jnp.full((8, 128), len_ref[0].astype(F32), F32)
    kvs[0:16, :] = total
    kvs[16:24, :] = fill
    put, kv_pair_arrived = group("kv pair", kvs)
    put(kvs, kvin, twin)
    kv_pair_arrived()
    row8 = lax.broadcasted_iota(jnp.int32, (8, 128), 0)
    msgs[y, 0:16, :] = total + kvin[0:16, :]
    msgs[y, 16:24, :] = jnp.where(row8 == core, fill, kvin[16:24, :])
    put, messages_arrived = group("messages", msgs.at[0:3])
    for d in (2, 3, 1):
        put(msgs.at[y], msgs.at[y], device(z, lax.rem(y + d, NY), core, x, h))

    cache_line_arrived()
    put, cache_relay_arrived = group("cache relay", kb.at[0:2])
    for buf in (kb, vb):
        put(buf.at[2], buf.at[3], twin)
    cache_twin_arrived()
    messages_arrived()
    cache_relay_arrived()

    scale = LOG2E / math.sqrt(128.0)
    place = lax.broadcasted_iota(jnp.int32, (1, 512), 1).astype(F32)
    bias, lengths = [], []
    for chip in (y, keys_y):
        pair = (msgs[chip, 16:17, :], msgs[chip, 17:18, :])
        lengths += [jnp.where(core == 0, *pair), jnp.where(core == 0, *pair[::-1])]
    for length in lengths:
        filled = jnp.concatenate([length] * 4, axis=1)
        bias.append(jnp.where(place < filled, 0.0, NEG))
    bias = jnp.concatenate(bias, axis=1)
    keys = kb[...].reshape(2048, 128)
    values = vb[...].reshape(2048, 128)
    diagonal = lax.broadcasted_iota(jnp.int32, (32, 128), 0) == lax.broadcasted_iota(jnp.int32, (32, 128), 1)
    row16 = lax.broadcasted_iota(jnp.int32, (16, 128), 0)

    def attend(j, new):
        queries = qb[j]
        scores = dot_t(queries, keys) * scale + bias
        top = jnp.max(scores, axis=1, keepdims=True)
        if new:
            new_keys = jnp.concatenate([msgs[i, 0:16, :] for i in (0, 2)], axis=0).astype(BF16)
            new_values = jnp.concatenate([msgs[i, 0:16, :] for i in (1, 3)], axis=0).astype(BF16)
            key_at = lax.broadcasted_iota(jnp.int32, (256, 32), 1) + z * 32
            row_at = lax.broadcasted_iota(jnp.int32, (256, 32), 0)
            fresh = jnp.where(key_at <= row_at, dot_t(queries, new_keys) * scale, NEG)
            top = jnp.maximum(top, jnp.max(fresh, axis=1, keepdims=True))
        weight = jnp.exp2(scores - top)
        sums = jnp.sum(weight, axis=1, keepdims=True)
        mixed = dot(weight.astype(BF16), values)
        if new:
            weight = jnp.exp2(fresh - top)
            sums = sums + jnp.sum(weight, axis=1, keepdims=True)
            mixed = mixed + dot(weight.astype(BF16), new_values)
        shared = (mixed / sums).astype(BF16)
        level = top + jnp.log2(sums)
        for b in range(NZ):
            rows = slice(32 * b, 32 * b + 32)
            po[j, b, 0:32, :] = shared[rows]
            line = jnp.sum(jnp.where(diagonal, level[rows], 0.0), axis=0, keepdims=True)
            high = line.astype(BF16).astype(F32)
            mid = (line - high).astype(BF16).astype(F32)
            low = line - high - mid
            po[j, b, 32:48, :] = jnp.where(row16 == 0, high, jnp.where(row16 == 1, mid, low)).astype(BF16)

    put0, partials0_arrived = group("partials 0", pod.at[0, 0:7])
    put1, partials1_arrived = group("partials 1", pod.at[1])
    heads1_arrived()
    attend(1, False)
    for d in (4, 3, 5, 2, 6, 1, 7, 0):
        to, dev = zdev(d, heads_y)
        put1(po.at[1, to], pod.at[1, z], dev)
    heads0_arrived()
    attend(0, True)
    for d in (4, 3, 5, 2, 6, 1, 7):
        to, dev = zdev(d)
        put0(po.at[0, to], pod.at[0, z], dev)
    pod[0, z] = po[0, z]
    partials0_arrived()
    partials1_arrived()

    levels, parts = [], []
    for j in range(2):
        for b in range(NZ):
            rows = pod[j, b, 32:48, :].astype(F32)
            line = rows[0:1] + rows[1:2] + rows[2:3]
            spread = jnp.where(diagonal, jnp.broadcast_to(line, (32, 128)), 0.0)
            levels.append(jnp.sum(spread, axis=1, keepdims=True))
            parts.append(pod[j, b, 0:32, :].astype(F32))
    top = functools.reduce(jnp.maximum, levels)
    shares = [jnp.exp2(one - top) for one in levels]
    whole = functools.reduce(jnp.add, shares)
    merged = functools.reduce(jnp.add, [part * share for part, share in zip(parts, shares)])

    own_lanes = pl.ds(pl.multiple_of((y % 2) * 128, 128), 128)
    att[0, zrows, own_lanes] = (merged / whole).astype(BF16)
    put, attended_arrived = group("attended", att.at[0, 0:240])
    attended = att.at[0, zrows, own_lanes]
    for d in (4, 3, 5, 2, 6, 1, 7, 0):
        put(attended, attended, zdev(d, keys_y)[1])
    for d in (4, 3, 5, 2, 6, 1, 7):
        put(attended, attended, zdev(d)[1])
    out_weights_arrived()
    attended_arrived()
    put, across_arrived = group("across", att.at[1])
    put(att.at[0], att.at[1], twin)

    first = dot(att[0], wo[core])
    across_arrived()
    put, plane_arrived = group("plane", p7.at[0:15])
    both = (first + dot(att[1], wo[other])).astype(BF16)
    o2s[0] = both[:, :128]
    o2s[1] = both[:, 128:]
    for e, dh in ((0, 1), (1, 1), (1, 0), (0, 0)):
        for dx in (2, 1, 3, 0):
            if (e, dh, dx) == (0, 0, 0):
                continue
            to_x, to_h = lax.rem(x + dx, NX), lax.rem(h + dh, NH)
            rows = pl.ds(pl.multiple_of((to_x * NH + to_h) * 32, 32), 32)
            put(o2s.at[e, rows], p7.at[2 * tp + e], device(z, (y, heads_y)[e], core, to_x, to_h))
    p7[2 * tp] = o2s[0, own_rows, :]
    for d in range(1, 8):
        hidden_y(d).wait_send()
    for d in range(1, NX):
        hidden_x(d, x_rows).wait_send()
    for wait in sent[:-1]:
        wait()
    plane_arrived()
    result = p7[0].astype(F32)
    for b in range(1, 16):
        result = result + p7[b].astype(F32)
    out_ref[...] = result
    sent[-1]()


def per_device(hidden_in, w_query, w_key, w_value, w_out, cache_keys, cache_values, prefix_lengths):
    dma = pltpu.SemaphoreType.DMA
    vmem = pltpu.VMEM
    in_hbm = pl.BlockSpec(memory_space=pltpu.HBM)
    return pl.pallas_call(
        kernel,
        out_shape=jax.ShapeDtypeStruct((32, 128), F32),
        in_specs=[in_hbm] * 7 + [pl.BlockSpec(memory_space=pltpu.SMEM)],
        out_specs=pl.BlockSpec(memory_space=pltpu.VMEM),
        scratch_shapes=[
            vmem((256, 512), BF16), vmem((128, 1024), BF16), vmem((2, 128, 128), BF16), vmem((1024, 128), BF16),
            vmem((4, 128, 256), BF16), vmem((4, 128, 128), BF16), vmem((2, 256, 256), BF16),
            vmem((4, 512, 128), BF16), vmem((4, 512, 128), BF16),
            vmem((2, 256, 128), F32), vmem((256, 128), F32), vmem((256, 128), F32),
            vmem((24, 128), F32), vmem((24, 128), F32),
            vmem((8, 32, 128), F32), vmem((8, 32, 128), F32), vmem((8, 16, 128), F32), vmem((8, 16, 128), F32),
            vmem((2, 256, 128), BF16), vmem((4, 24, 128), F32),
            vmem((2, 8, 48, 128), BF16), vmem((2, 8, 48, 128), BF16),
            vmem((2, 256, 256), BF16), vmem((2, 256, 128), BF16), vmem((16, 32, 128), BF16),
            dma((7,)), dma((len(GROUPS),)), dma((len(GROUPS),)), dma((8,)), dma((8,)), dma((4,)), dma((4,)),
            pltpu.SemaphoreType.REGULAR((5,)),
        ],
        compiler_params=pltpu.CompilerParams(
            collective_id=0, has_side_effects=True, vmem_limit_bytes=56 * 1024 * 1024
        ),
        cost_estimate=pl.CostEstimate(flops=1_000_000_000, bytes_accessed=2_000_000, transcendentals=1_100_000),
        name="attention_block",
    )(
        hidden_in, w_query, w_key, w_value, w_out,
        cache_keys.reshape(cache_keys.shape[0], 128), cache_values.reshape(cache_values.shape[0], 128),
        prefix_lengths,
    )


def solution(mesh):
    placed = (
        P("tp", "ctx"),
        P("ctx", "tp"),
        P("ctx", "tp"),
        P("ctx", "tp"),
        P("tp", "ctx"),
        P("ctx", "tp", None),
        P("ctx", "tp", None),
        P("ctx"),
    )
    return jax.shard_map(
        per_device, mesh=mesh, in_specs=placed, out_specs=P("tp", "ctx"), check_vma=False
    )
```

```python
import functools
import math

import jax
import jax.numpy as jnp
from jax import lax
from jax.experimental import pallas as pl
from jax.experimental.pallas import tpu as pltpu
from jax.sharding import PartitionSpec as P

MESH = pl.DeviceIdType.MESH
F32 = jnp.float32
BF16 = jnp.bfloat16
NZ, NY, NX, NH = 8, 4, 4, 2
LOG2E = 1.0 / math.log(2.0)
NEG = -1e30
KEYS_WITH = 1
HEADS_WITH = 2
GROUPS = (
    "query weights", "kv weights", "cache twin", "cache line", "cache relay", "length twin", "length line",
    "length relay", "out weights", "pair",
    "queries", "kv pair", "kv", "heads 0", "heads 1", "messages", "partials 0", "partials 1", "levels 0", "levels 1", "attended", "across",
    "plane",
)


def coords():
    c = lax.axis_index("ctx")
    t = lax.axis_index("tp")
    return c // 8, (c // 2) % 4, c % 2, t // 2, t % 2


def device(z, y, core, x, h):
    return ((z * NY + y) * 2 + core, x * NH + h)


def dot(a, b):
    return jnp.dot(a, b, preferred_element_type=F32)


def dot_t(a, b):
    return lax.dot_general(a, b, (((1,), (1,)), ((), ())), preferred_element_type=F32)


def kernel(
    hid_ref, wq_ref, wk_ref, wv_ref, wo_ref, ck_ref, cv_ref, len_ref, out_ref,
    hs, wqs, wkvs, wos, wq, wkv, wo, kb, vb, yp, yin, yk, kvs, kvin, fill, p2s, p2d, p2k, p2e, qb, msgs,
    po, pod, pl_s, pl_d, att, o2s, p7, loc, ssem, rsem, s_hy, r_hy, s_hx, r_hx, known,
):
    z, y, core, x, h = coords()
    other = 1 - core
    yf = h * NY + y
    tp = x * NH + h
    own_rows = pl.ds(pl.multiple_of(tp * 32, 32), 32)
    own_cols = pl.ds(pl.multiple_of(y * 128, 128), 128)
    zrows = pl.ds(pl.multiple_of(z * 32, 32), 32)

    def xor_y(bits):
        if bits == 1:
            return y + 1 - 2 * (y % 2)
        return lax.rem(y + 2, NY)

    keys_y, heads_y = xor_y(KEYS_WITH), xor_y(HEADS_WITH)
    twin = device(z, y, other, x, h)

    def remote(src, dst, ssem, rsem, dev):
        return pltpu.make_async_remote_copy(
            src_ref=src, dst_ref=dst, send_sem=ssem, recv_sem=rsem, device_id=dev, device_id_type=MESH
        )

    sent = []

    def group(name, size):
        index = GROUPS.index(name)

        def put(src, dst, dev):
            remote(src, dst, ssem.at[index], rsem.at[index], dev).start()

        def arrived():
            remote(size, size, ssem.at[index], rsem.at[index], twin).wait_recv()

        sent.append(lambda: remote(size, size, ssem.at[index], rsem.at[index], twin).wait_send())
        return put, arrived

    local = [
        pltpu.make_async_copy(hid_ref, hs.at[own_rows, own_cols], loc.at[0]),
        pltpu.make_async_copy(wq_ref, wqs, loc.at[1]),
        pltpu.make_async_copy(wk_ref, wkvs.at[0], loc.at[2]),
        pltpu.make_async_copy(wv_ref, wkvs.at[1], loc.at[3]),
        pltpu.make_async_copy(ck_ref, kb.at[0], loc.at[4]),
        pltpu.make_async_copy(cv_ref, vb.at[0], loc.at[5]),
        pltpu.make_async_copy(wo_ref, wos, loc.at[6]),
    ]
    for copy in local:
        copy.start()

    barrier = pltpu.get_barrier_semaphore()

    def zdev(d, at_y=y):
        to = lax.rem(z + d, NZ)
        return to, device(to, at_y, core, x, h)

    def yring(d):
        to = lax.rem(yf + d, 8)
        return device(z, to % 4, core, x, to // 4)

    near = [yring(d) for d in (4, 3, 5, 2, 6, 1, 7)]
    near += [device(z, y, core, lax.rem(x + d, NX), h) for d in (2, 1, 3)]
    near += [zdev(1)[1], zdev(7)[1], twin]
    for dev in near:
        pl.semaphore_signal(barrier, inc=1, device_id=dev, device_id_type=MESH)
    pl.semaphore_wait(barrier, len(near))

    def tell(i, d):
        pl.semaphore_signal(known.at[i], inc=1, device_id=zdev(d)[1], device_id_type=MESH)

    def block(d):
        at = lax.rem(yf + 8 - d, 8)
        rows = pl.ds(pl.multiple_of((x * NH + at // 4) * 32, 32), 32)
        return hs.at[rows, pl.ds(pl.multiple_of((at % 4) * 128, 128), 128)]

    def hidden_y(d):
        return remote(block(0), block(0), s_hy.at[d], r_hy.at[d], yring(d))

    def hidden_x(d, view):
        return remote(view, view, s_hx.at[d], r_hx.at[d], device(z, y, core, lax.rem(x + d, NX), h))

    def forward(d):
        for dx in (2, 1, 3):
            hidden_x(dx, block(d)).start()

    x_rows = hs.at[pl.ds(pl.multiple_of(x * 64, 64), 64)]
    local[0].wait()
    for d in (4, 3, 5, 2, 6, 1, 7):
        hidden_y(d).start()
    forward(0)
    tell(0, 1)
    tell(1, 7)

    put, query_weights_arrived = group("query weights", wq.at[0:3])
    local[1].wait()
    for d in (2, 3, 1):
        to = lax.rem(y + d, NY)
        put(wqs.at[:, pl.ds(pl.multiple_of(to * 256, 256), 256)], wq.at[y], device(z, to, core, x, h))
    wq[y] = wqs[:, pl.ds(pl.multiple_of(y * 256, 256), 256)]

    fill[0:1, :] = jnp.full((1, 128), len_ref[0].astype(F32), F32)
    put, length_twin_arrived = group("length twin", fill.at[0:1])
    put(fill.at[0:1], fill.at[1:2], twin)
    put, cache_twin_arrived = group("cache twin", kb.at[0:2])
    for i, buf in enumerate((kb, vb)):
        local[4 + i].wait()
        put(buf.at[0], buf.at[1], twin)
    for copy in local[2:4]:
        copy.wait()
    wkv[y] = wkvs[y % 2]

    for d in (1, 7, 2, 6):
        hidden_y(d).wait_recv()
        forward(d)
    for i in range(2):
        pl.semaphore_wait(known.at[i], 1)
    tell(2, 1)
    tell(3, 7)
    tell(4, 2)
    for d in (3, 5, 4):
        hidden_y(d).wait_recv()
        forward(d)

    put, kv_weights_arrived = group("kv weights", wkv.at[0:3])
    for d in (2, 3, 1):
        to = lax.rem(y + d, NY)
        put(wkvs.at[to % 2], wkv.at[y], device(z, to, core, x, h))

    query_weights_arrived()
    put, length_line_arrived = group("length line", fill.at[0:1])
    put(fill.at[0:1], fill.at[2:3], device(z, keys_y, core, x, h))
    put, cache_line_arrived = group("cache line", kb.at[0:2])
    for buf in (kb, vb):
        put(buf.at[0], buf.at[2], device(z, keys_y, core, x, h))
    wqf = wq[...].reshape(512, 256)

    def project(block):
        rows = pl.ds(pl.multiple_of(block * 64, 64), 64)
        both = dot(hs[rows, :], wqf)
        yp[0, rows, :] = both[:, :128]
        yp[1, rows, :] = both[:, 128:]

    project(x)
    for d in (1, 3, 2):
        hidden_x(d, x_rows).wait_recv()
        project(lax.rem(x + NX - d, NX))

    put, pair_arrived = group("pair", yin)
    put(yp.at[other], yin, twin)

    put, out_weights_arrived = group("out weights", wo.at[0])
    local[6].wait()
    for pair_core in range(2):
        for chip in range(2):
            def rows_of(at):
                return pl.ds(pl.multiple_of((at // 2) * 512 + 256 * chip + 128 * pair_core, 128), 128)

            there = wo.at[pair_core, pl.ds(128 * chip, 128)]
            put(wos.at[rows_of(heads_y)], there.at[:, pl.ds(128, 128)], device(z, heads_y, core, x, h))
            wo[pair_core, 128 * chip : 128 * chip + 128, 0:128] = wos[rows_of(y), :]

    pair_arrived()
    for b in range(NZ):
        rows = slice(32 * b, 32 * b + 32)
        p2s[b] = yp[core, rows, :] + yin[rows, :]

    for i in range(2, 5):
        pl.semaphore_wait(known.at[i], 1)
    put, queries_arrived = group("queries", p2d.at[0:7])
    for d in (4, 3, 5, 2, 6, 1, 7):
        to, dev = zdev(d)
        put(p2s.at[to], p2d.at[z], dev)
    p2d[z] = p2s[z]

    kv_weights_arrived()
    yk[...] = dot(hs[...], wkv[...].reshape(512, 128))
    half = 16 * (y // 2)
    for b in range(NZ):
        p2k[b] = yk[pl.ds(pl.multiple_of(32 * b + half, 16), 16), :]
    put, kv_arrived = group("kv", p2e.at[0:7])
    for d in (4, 3, 5, 2, 6, 1, 7):
        to, dev = zdev(d)
        put(p2k.at[to], p2e.at[z], dev)
    p2e[z] = p2k[z]

    queries_arrived()
    total = p2d[0]
    for b in range(1, NZ):
        total = total + p2d[b]
    qb[0, zrows, :] = total.astype(BF16)
    put0, heads0_arrived = group("heads 0", qb.at[0, 0:224])
    put1, heads1_arrived = group("heads 1", qb.at[1])
    for d in (4, 3, 5, 2, 6, 1, 7, 0):
        put1(qb.at[0, zrows], qb.at[1, zrows], zdev(d, heads_y)[1])
    for d in (4, 3, 5, 2, 6, 1, 7):
        put0(qb.at[0, zrows], qb.at[0, zrows], zdev(d)[1])

    kv_arrived()
    total = p2e[0]
    for b in range(1, NZ):
        total = total + p2e[b]
    kvs[...] = total
    put, kv_pair_arrived = group("kv pair", kvs)
    put(kvs, kvin, twin)
    kv_pair_arrived()
    msgs[y] = total + kvin[...]
    put, messages_arrived = group("messages", msgs.at[0:3])
    for d in (2, 3, 1):
        put(msgs.at[y], msgs.at[y], device(z, lax.rem(y + d, NY), core, x, h))

    cache_line_arrived()
    length_line_arrived()
    put, length_relay_arrived = group("length relay", fill.at[0:1])
    put(fill.at[2:3], fill.at[3:4], twin)
    put, cache_relay_arrived = group("cache relay", kb.at[0:2])
    for buf in (kb, vb):
        put(buf.at[2], buf.at[3], twin)
    length_twin_arrived()
    cache_twin_arrived()
    length_relay_arrived()
    cache_relay_arrived()

    scale = LOG2E / math.sqrt(128.0)
    place = lax.broadcasted_iota(jnp.int32, (1, 512), 1).astype(F32)
    bias = []
    for slot in range(4):
        filled = jnp.concatenate([fill[slot : slot + 1, :]] * 4, axis=1)
        bias.append(jnp.where(place < filled, 0.0, NEG))
    bias = jnp.concatenate(bias, axis=1)
    keys = kb[...].reshape(2048, 128)
    values = vb[...].reshape(2048, 128)
    diagonal = lax.broadcasted_iota(jnp.int32, (32, 128), 0) == lax.broadcasted_iota(jnp.int32, (32, 128), 1)

    def attend(j, new):
        queries = qb[j]
        scores = dot_t(queries, keys) * scale + bias
        top = jnp.max(scores, axis=1, keepdims=True)
        weight = jnp.exp2(scores - top)
        sums = jnp.sum(weight, axis=1, keepdims=True)
        mixed = dot(weight.astype(BF16), values)
        if new:
            messages_arrived()
            new_keys = jnp.concatenate([msgs[i] for i in (0, 2)], axis=0).astype(BF16)
            new_values = jnp.concatenate([msgs[i] for i in (1, 3)], axis=0).astype(BF16)
            key_at = lax.broadcasted_iota(jnp.int32, (256, 32), 1) + z * 32
            row_at = lax.broadcasted_iota(jnp.int32, (256, 32), 0)
            fresh = jnp.where(key_at <= row_at, dot_t(queries, new_keys) * scale, NEG)
            raised = jnp.maximum(top, jnp.max(fresh, axis=1, keepdims=True))
            shrink = jnp.exp2(top - raised)
            weight = jnp.exp2(fresh - raised)
            sums = sums * shrink + jnp.sum(weight, axis=1, keepdims=True)
            mixed = mixed * shrink + dot(weight.astype(BF16), new_values)
            top = raised
        shared = (mixed / sums).astype(BF16)
        level = top + jnp.log2(sums)
        for b in range(NZ):
            rows = slice(32 * b, 32 * b + 32)
            po[j, b] = shared[rows]
            line = jnp.sum(jnp.where(diagonal, level[rows], 0.0), axis=0, keepdims=True)
            pl_s[j, b : b + 1, :] = line

    put0, partials0_arrived = group("partials 0", pod.at[0, 0:7])
    put1, partials1_arrived = group("partials 1", pod.at[1])
    putl0, levels0_arrived = group("levels 0", pl_d.at[0, 0:7])
    putl1, levels1_arrived = group("levels 1", pl_d.at[1])
    heads1_arrived()
    attend(1, False)
    for d in (4, 3, 5, 2, 6, 1, 7, 0):
        to, dev = zdev(d, heads_y)
        put1(po.at[1, to], pod.at[1, z], dev)
        putl1(pl_s.at[1, pl.ds(to, 1)], pl_d.at[1, pl.ds(z, 1)], dev)
    heads0_arrived()
    attend(0, True)
    for d in (4, 3, 5, 2, 6, 1, 7):
        to, dev = zdev(d)
        put0(po.at[0, to], pod.at[0, z], dev)
        putl0(pl_s.at[0, pl.ds(to, 1)], pl_d.at[0, pl.ds(z, 1)], dev)
    pod[0, z] = po[0, z]
    pl_d[0, pl.ds(z, 1), :] = pl_s[0, pl.ds(z, 1), :]
    for arrived in (partials0_arrived, levels0_arrived, partials1_arrived, levels1_arrived):
        arrived()

    levels, parts = [], []
    for j in range(2):
        for b in range(NZ):
            spread = jnp.where(diagonal, jnp.broadcast_to(pl_d[j, b : b + 1, :], (32, 128)), 0.0)
            levels.append(jnp.sum(spread, axis=1, keepdims=True))
            parts.append(pod[j, b].astype(F32))
    top = functools.reduce(jnp.maximum, levels)
    shares = [jnp.exp2(one - top) for one in levels]
    whole = functools.reduce(jnp.add, shares)
    merged = functools.reduce(jnp.add, [part * share for part, share in zip(parts, shares)])

    own_lanes = pl.ds(pl.multiple_of((y % 2) * 128, 128), 128)
    att[0, zrows, own_lanes] = (merged / whole).astype(BF16)
    put, attended_arrived = group("attended", att.at[0, 0:240])
    attended = att.at[0, zrows, own_lanes]
    for d in (4, 3, 5, 2, 6, 1, 7, 0):
        put(attended, attended, zdev(d, keys_y)[1])
    for d in (4, 3, 5, 2, 6, 1, 7):
        put(attended, attended, zdev(d)[1])
    out_weights_arrived()
    attended_arrived()
    put, across_arrived = group("across", att.at[1])
    put(att.at[0], att.at[1], twin)

    first = dot(att[0], wo[core])
    across_arrived()
    put, plane_arrived = group("plane", p7.at[0:15])
    both = (first + dot(att[1], wo[other])).astype(BF16)
    o2s[0] = both[:, :128]
    o2s[1] = both[:, 128:]
    for e, dh in ((0, 1), (1, 1), (1, 0), (0, 0)):
        for dx in (2, 1, 3, 0):
            if (e, dh, dx) == (0, 0, 0):
                continue
            to_x, to_h = lax.rem(x + dx, NX), lax.rem(h + dh, NH)
            rows = pl.ds(pl.multiple_of((to_x * NH + to_h) * 32, 32), 32)
            put(o2s.at[e, rows], p7.at[2 * tp + e], device(z, (y, heads_y)[e], core, to_x, to_h))
    p7[2 * tp] = o2s[0, own_rows, :]
    for d in range(1, 8):
        hidden_y(d).wait_send()
    for d in range(1, NX):
        hidden_x(d, x_rows).wait_send()
    for wait in sent[:-1]:
        wait()
    plane_arrived()
    result = p7[0].astype(F32)
    for b in range(1, 16):
        result = result + p7[b].astype(F32)
    out_ref[...] = result
    sent[-1]()


def per_device(hidden_in, w_query, w_key, w_value, w_out, cache_keys, cache_values, prefix_lengths):
    dma = pltpu.SemaphoreType.DMA
    vmem = pltpu.VMEM
    in_hbm = pl.BlockSpec(memory_space=pltpu.HBM)
    return pl.pallas_call(
        kernel,
        out_shape=jax.ShapeDtypeStruct((32, 128), F32),
        in_specs=[in_hbm] * 7 + [pl.BlockSpec(memory_space=pltpu.SMEM)],
        out_specs=pl.BlockSpec(memory_space=pltpu.VMEM),
        scratch_shapes=[
            vmem((256, 512), BF16), vmem((128, 1024), BF16), vmem((2, 128, 128), BF16), vmem((1024, 128), BF16),
            vmem((4, 128, 256), BF16), vmem((4, 128, 128), BF16), vmem((2, 256, 256), BF16),
            vmem((4, 512, 128), BF16), vmem((4, 512, 128), BF16),
            vmem((2, 256, 128), F32), vmem((256, 128), F32), vmem((256, 128), F32),
            vmem((16, 128), F32), vmem((16, 128), F32), vmem((8, 128), F32),
            vmem((8, 32, 128), F32), vmem((8, 32, 128), F32), vmem((8, 16, 128), F32), vmem((8, 16, 128), F32),
            vmem((2, 256, 128), BF16), vmem((4, 16, 128), F32),
            vmem((2, 8, 32, 128), BF16), vmem((2, 8, 32, 128), BF16),
            vmem((2, 8, 128), F32), vmem((2, 8, 128), F32),
            vmem((2, 256, 256), BF16), vmem((2, 256, 128), BF16), vmem((16, 32, 128), BF16),
            dma((7,)), dma((len(GROUPS),)), dma((len(GROUPS),)), dma((8,)), dma((8,)), dma((4,)), dma((4,)),
            pltpu.SemaphoreType.REGULAR((5,)),
        ],
        compiler_params=pltpu.CompilerParams(
            collective_id=0, has_side_effects=True, vmem_limit_bytes=56 * 1024 * 1024
        ),
        cost_estimate=pl.CostEstimate(flops=1_000_000_000, bytes_accessed=2_000_000, transcendentals=1_100_000),
        name="attention_block",
    )(
        hidden_in, w_query, w_key, w_value, w_out,
        cache_keys.reshape(cache_keys.shape[0], 128), cache_values.reshape(cache_values.shape[0], 128),
        prefix_lengths,
    )


def solution(mesh):
    placed = (
        P("tp", "ctx"),
        P("ctx", "tp"),
        P("ctx", "tp"),
        P("ctx", "tp"),
        P("tp", "ctx"),
        P("ctx", "tp", None),
        P("ctx", "tp", None),
        P("ctx"),
    )
    return jax.shard_map(
        per_device, mesh=mesh, in_specs=placed, out_specs=P("tp", "ctx"), check_vma=False
    )
```

```python
import functools
import math

import jax
import jax.numpy as jnp
from jax import lax
from jax.experimental import pallas as pl
from jax.experimental.pallas import tpu as pltpu
from jax.sharding import PartitionSpec as P

MESH = pl.DeviceIdType.MESH
F32 = jnp.float32
BF16 = jnp.bfloat16
NZ, NY, NX, NH = 8, 4, 4, 2
LOG2E = 1.0 / math.log(2.0)
NEG = -1e30
KEYS_WITH = 1
HEADS_WITH = 2
GROUPS = (
    "query weights", "kv weights", "cache twin", "cache line", "cache relay", "length twin", "length line",
    "length relay", "out weights", "pair",
    "queries", "kv pair", "kv", "heads 0", "heads 1", "messages", "partials 0", "partials 1", "levels 0", "levels 1", "attended", "across",
    "plane",
)


def coords():
    c = lax.axis_index("ctx")
    t = lax.axis_index("tp")
    return c // 8, (c // 2) % 4, c % 2, t // 2, t % 2


def device(z, y, core, x, h):
    return ((z * NY + y) * 2 + core, x * NH + h)


def dot(a, b):
    return jnp.dot(a, b, preferred_element_type=F32)


def dot_t(a, b):
    return lax.dot_general(a, b, (((1,), (1,)), ((), ())), preferred_element_type=F32)


def kernel(
    hid_ref, wq_ref, wk_ref, wv_ref, wo_ref, ck_ref, cv_ref, len_ref, out_ref,
    hs, wqs, wkvs, wos, wq, wkv, wo, kb, vb, yp, yin, yk, kvs, kvin, fill, p2s, p2d, p2k, p2e, qb, msgs,
    po, pod, pl_s, pl_d, att, o2s, p7, loc, ssem, rsem, s_hy, r_hy, s_hx, r_hx, known,
):
    z, y, core, x, h = coords()
    other = 1 - core
    yf = h * NY + y
    tp = x * NH + h
    own_rows = pl.ds(pl.multiple_of(tp * 32, 32), 32)
    own_cols = pl.ds(pl.multiple_of(y * 128, 128), 128)
    zrows = pl.ds(pl.multiple_of(z * 32, 32), 32)

    def xor_y(bits):
        if bits == 1:
            return y + 1 - 2 * (y % 2)
        return lax.rem(y + 2, NY)

    keys_y, heads_y = xor_y(KEYS_WITH), xor_y(HEADS_WITH)
    twin = device(z, y, other, x, h)

    def remote(src, dst, ssem, rsem, dev):
        return pltpu.make_async_remote_copy(
            src_ref=src, dst_ref=dst, send_sem=ssem, recv_sem=rsem, device_id=dev, device_id_type=MESH
        )

    sent = []

    def group(name, size):
        index = GROUPS.index(name)

        def put(src, dst, dev):
            remote(src, dst, ssem.at[index], rsem.at[index], dev).start()

        def arrived():
            remote(size, size, ssem.at[index], rsem.at[index], twin).wait_recv()

        sent.append(lambda: remote(size, size, ssem.at[index], rsem.at[index], twin).wait_send())
        return put, arrived

    local = [
        pltpu.make_async_copy(hid_ref, hs.at[own_rows, own_cols], loc.at[0]),
        pltpu.make_async_copy(wq_ref, wqs, loc.at[1]),
        pltpu.make_async_copy(wk_ref, wkvs.at[0], loc.at[2]),
        pltpu.make_async_copy(wv_ref, wkvs.at[1], loc.at[3]),
        pltpu.make_async_copy(ck_ref, kb.at[0], loc.at[4]),
        pltpu.make_async_copy(cv_ref, vb.at[0], loc.at[5]),
        pltpu.make_async_copy(wo_ref, wos, loc.at[6]),
    ]
    barrier = pltpu.get_barrier_semaphore()

    def zdev(d, at_y=y):
        to = lax.rem(z + d, NZ)
        return to, device(to, at_y, core, x, h)

    def yring(d):
        to = lax.rem(yf + d, 8)
        return device(z, to % 4, core, x, to // 4)

    near = [yring(d) for d in (4, 3, 5, 2, 6, 1, 7)]
    near += [device(z, y, core, lax.rem(x + d, NX), h) for d in (2, 1, 3)]
    near += [zdev(1)[1], zdev(7)[1], twin]
    for dev in near:
        pl.semaphore_signal(barrier, inc=1, device_id=dev, device_id_type=MESH)
    for copy in local:
        copy.start()
    pl.semaphore_wait(barrier, len(near))

    def tell(i, d):
        pl.semaphore_signal(known.at[i], inc=1, device_id=zdev(d)[1], device_id_type=MESH)

    def block(d):
        at = lax.rem(yf + 8 - d, 8)
        rows = pl.ds(pl.multiple_of((x * NH + at // 4) * 32, 32), 32)
        return hs.at[rows, pl.ds(pl.multiple_of((at % 4) * 128, 128), 128)]

    def hidden_y(d):
        return remote(block(0), block(0), s_hy.at[d], r_hy.at[d], yring(d))

    def hidden_x(d, view):
        return remote(view, view, s_hx.at[d], r_hx.at[d], device(z, y, core, lax.rem(x + d, NX), h))

    def forward(d):
        for dx in (2, 1, 3):
            hidden_x(dx, block(d)).start()

    x_rows = hs.at[pl.ds(pl.multiple_of(x * 64, 64), 64)]
    local[0].wait()
    for d in (4, 3, 5, 2, 6, 1, 7):
        hidden_y(d).start()
    forward(0)
    tell(0, 1)
    tell(1, 7)

    put, query_weights_arrived = group("query weights", wq.at[0:3])
    local[1].wait()
    for d in (2, 3, 1):
        to = lax.rem(y + d, NY)
        put(wqs.at[:, pl.ds(pl.multiple_of(to * 256, 256), 256)], wq.at[y], device(z, to, core, x, h))
    wq[y] = wqs[:, pl.ds(pl.multiple_of(y * 256, 256), 256)]

    fill[0:1, :] = jnp.full((1, 128), len_ref[0].astype(F32), F32)
    put, length_twin_arrived = group("length twin", fill.at[0:1])
    put(fill.at[0:1], fill.at[1:2], twin)
    put, cache_twin_arrived = group("cache twin", kb.at[0:2])
    for i, buf in enumerate((kb, vb)):
        local[4 + i].wait()
        put(buf.at[0], buf.at[1], twin)
    for copy in local[2:4]:
        copy.wait()
    wkv[y] = wkvs[y % 2]

    for d in (1, 7, 2, 6):
        hidden_y(d).wait_recv()
        forward(d)
    for i in range(2):
        pl.semaphore_wait(known.at[i], 1)
    tell(2, 1)
    tell(3, 7)
    tell(4, 2)
    for d in (3, 5, 4):
        hidden_y(d).wait_recv()
        forward(d)

    put, kv_weights_arrived = group("kv weights", wkv.at[0:3])
    for d in (2, 3, 1):
        to = lax.rem(y + d, NY)
        put(wkvs.at[to % 2], wkv.at[y], device(z, to, core, x, h))

    put, length_line_arrived = group("length line", fill.at[0:1])
    put(fill.at[0:1], fill.at[2:3], device(z, keys_y, core, x, h))
    put, cache_line_arrived = group("cache line", kb.at[0:2])
    for buf in (kb, vb):
        put(buf.at[0], buf.at[2], device(z, keys_y, core, x, h))

    query_weights_arrived()
    put, out_weights_arrived = group("out weights", wo.at[0])
    local[6].wait()
    for pair_core in range(2):
        for chip in range(2):
            def rows_of(at):
                return pl.ds(pl.multiple_of((at // 2) * 512 + 256 * chip + 128 * pair_core, 128), 128)

            there = wo.at[pair_core, pl.ds(128 * chip, 128)]
            put(wos.at[rows_of(heads_y)], there.at[:, pl.ds(128, 128)], device(z, heads_y, core, x, h))
            wo[pair_core, 128 * chip : 128 * chip + 128, 0:128] = wos[rows_of(y), :]

    wqf = wq[...].reshape(512, 256)

    def project(block):
        rows = pl.ds(pl.multiple_of(block * 64, 64), 64)
        both = dot(hs[rows, :], wqf)
        yp[0, rows, :] = both[:, :128]
        yp[1, rows, :] = both[:, 128:]

    project(x)
    for d in (1, 3, 2):
        hidden_x(d, x_rows).wait_recv()
        project(lax.rem(x + NX - d, NX))

    put, pair_arrived = group("pair", yin)
    put(yp.at[other], yin, twin)

    pair_arrived()
    for b in range(NZ):
        rows = slice(32 * b, 32 * b + 32)
        p2s[b] = yp[core, rows, :] + yin[rows, :]

    for i in range(2, 5):
        pl.semaphore_wait(known.at[i], 1)
    put, queries_arrived = group("queries", p2d.at[0:7])
    for d in (4, 3, 5, 2, 6, 1, 7):
        to, dev = zdev(d)
        put(p2s.at[to], p2d.at[z], dev)
    p2d[z] = p2s[z]

    kv_weights_arrived()
    yk[...] = dot(hs[...], wkv[...].reshape(512, 128))
    half = 16 * (y // 2)
    for b in range(NZ):
        p2k[b] = yk[pl.ds(pl.multiple_of(32 * b + half, 16), 16), :]
    put, kv_arrived = group("kv", p2e.at[0:7])
    for d in (4, 3, 5, 2, 6, 1, 7):
        to, dev = zdev(d)
        put(p2k.at[to], p2e.at[z], dev)
    p2e[z] = p2k[z]

    queries_arrived()
    total = p2d[0]
    for b in range(1, NZ):
        total = total + p2d[b]
    qb[0, zrows, :] = total.astype(BF16)
    put0, heads0_arrived = group("heads 0", qb.at[0, 0:224])
    put1, heads1_arrived = group("heads 1", qb.at[1])
    for d in (4, 3, 5, 2, 6, 1, 7, 0):
        put1(qb.at[0, zrows], qb.at[1, zrows], zdev(d, heads_y)[1])
    for d in (4, 3, 5, 2, 6, 1, 7):
        put0(qb.at[0, zrows], qb.at[0, zrows], zdev(d)[1])

    kv_arrived()
    total = p2e[0]
    for b in range(1, NZ):
        total = total + p2e[b]
    kvs[...] = total
    put, kv_pair_arrived = group("kv pair", kvs)
    put(kvs, kvin, twin)
    kv_pair_arrived()
    msgs[y] = total + kvin[...]
    put, messages_arrived = group("messages", msgs.at[0:3])
    for d in (2, 3, 1):
        put(msgs.at[y], msgs.at[y], device(z, lax.rem(y + d, NY), core, x, h))

    cache_line_arrived()
    length_line_arrived()
    put, length_relay_arrived = group("length relay", fill.at[0:1])
    put(fill.at[2:3], fill.at[3:4], twin)
    put, cache_relay_arrived = group("cache relay", kb.at[0:2])
    for buf in (kb, vb):
        put(buf.at[2], buf.at[3], twin)
    length_twin_arrived()
    cache_twin_arrived()
    length_relay_arrived()
    cache_relay_arrived()

    scale = LOG2E / math.sqrt(128.0)
    place = lax.broadcasted_iota(jnp.int32, (1, 512), 1).astype(F32)
    bias = []
    for slot in range(4):
        filled = jnp.concatenate([fill[slot : slot + 1, :]] * 4, axis=1)
        bias.append(jnp.where(place < filled, 0.0, NEG))
    bias = jnp.concatenate(bias, axis=1)
    keys = kb[...].reshape(2048, 128)
    values = vb[...].reshape(2048, 128)
    diagonal = lax.broadcasted_iota(jnp.int32, (32, 128), 0) == lax.broadcasted_iota(jnp.int32, (32, 128), 1)

    def attend(j, new):
        queries = qb[j]
        scores = dot_t(queries, keys) * scale + bias
        top = jnp.max(scores, axis=1, keepdims=True)
        weight = jnp.exp2(scores - top)
        sums = jnp.sum(weight, axis=1, keepdims=True)
        mixed = dot(weight.astype(BF16), values)
        if new:
            messages_arrived()
            new_keys = jnp.concatenate([msgs[i] for i in (0, 2)], axis=0).astype(BF16)
            new_values = jnp.concatenate([msgs[i] for i in (1, 3)], axis=0).astype(BF16)
            key_at = lax.broadcasted_iota(jnp.int32, (256, 32), 1) + z * 32
            row_at = lax.broadcasted_iota(jnp.int32, (256, 32), 0)
            fresh = jnp.where(key_at <= row_at, dot_t(queries, new_keys) * scale, NEG)
            raised = jnp.maximum(top, jnp.max(fresh, axis=1, keepdims=True))
            shrink = jnp.exp2(top - raised)
            weight = jnp.exp2(fresh - raised)
            sums = sums * shrink + jnp.sum(weight, axis=1, keepdims=True)
            mixed = mixed * shrink + dot(weight.astype(BF16), new_values)
            top = raised
        shared = (mixed / sums).astype(BF16)
        level = top + jnp.log2(sums)
        for b in range(NZ):
            rows = slice(32 * b, 32 * b + 32)
            po[j, b] = shared[rows]
            line = jnp.sum(jnp.where(diagonal, level[rows], 0.0), axis=0, keepdims=True)
            pl_s[j, b : b + 1, :] = line

    put0, partials0_arrived = group("partials 0", pod.at[0, 0:7])
    put1, partials1_arrived = group("partials 1", pod.at[1])
    putl0, levels0_arrived = group("levels 0", pl_d.at[0, 0:7])
    putl1, levels1_arrived = group("levels 1", pl_d.at[1])
    heads1_arrived()
    attend(1, False)
    for d in (4, 3, 5, 2, 6, 1, 7, 0):
        to, dev = zdev(d, heads_y)
        put1(po.at[1, to], pod.at[1, z], dev)
        putl1(pl_s.at[1, pl.ds(to, 1)], pl_d.at[1, pl.ds(z, 1)], dev)
    heads0_arrived()
    attend(0, True)
    for d in (4, 3, 5, 2, 6, 1, 7):
        to, dev = zdev(d)
        put0(po.at[0, to], pod.at[0, z], dev)
        putl0(pl_s.at[0, pl.ds(to, 1)], pl_d.at[0, pl.ds(z, 1)], dev)
    pod[0, z] = po[0, z]
    pl_d[0, pl.ds(z, 1), :] = pl_s[0, pl.ds(z, 1), :]
    for arrived in (partials0_arrived, levels0_arrived, partials1_arrived, levels1_arrived):
        arrived()

    levels, parts = [], []
    for j in range(2):
        for b in range(NZ):
            spread = jnp.where(diagonal, jnp.broadcast_to(pl_d[j, b : b + 1, :], (32, 128)), 0.0)
            levels.append(jnp.sum(spread, axis=1, keepdims=True))
            parts.append(pod[j, b].astype(F32))
    top = functools.reduce(jnp.maximum, levels)
    shares = [jnp.exp2(one - top) for one in levels]
    whole = functools.reduce(jnp.add, shares)
    merged = functools.reduce(jnp.add, [part * share for part, share in zip(parts, shares)])

    own_lanes = pl.ds(pl.multiple_of((y % 2) * 128, 128), 128)
    att[0, zrows, own_lanes] = (merged / whole).astype(BF16)
    put, attended_arrived = group("attended", att.at[0, 0:240])
    attended = att.at[0, zrows, own_lanes]
    for d in (4, 3, 5, 2, 6, 1, 7, 0):
        put(attended, attended, zdev(d, keys_y)[1])
    for d in (4, 3, 5, 2, 6, 1, 7):
        put(attended, attended, zdev(d)[1])
    out_weights_arrived()
    attended_arrived()
    put, across_arrived = group("across", att.at[1])
    put(att.at[0], att.at[1], twin)

    first = dot(att[0], wo[core])
    across_arrived()
    put, plane_arrived = group("plane", p7.at[0:15])
    both = (first + dot(att[1], wo[other])).astype(BF16)
    o2s[0] = both[:, :128]
    o2s[1] = both[:, 128:]
    for e, dh in ((0, 1), (1, 1), (1, 0), (0, 0)):
        for dx in (2, 1, 3, 0):
            if (e, dh, dx) == (0, 0, 0):
                continue
            to_x, to_h = lax.rem(x + dx, NX), lax.rem(h + dh, NH)
            rows = pl.ds(pl.multiple_of((to_x * NH + to_h) * 32, 32), 32)
            put(o2s.at[e, rows], p7.at[2 * tp + e], device(z, (y, heads_y)[e], core, to_x, to_h))
    p7[2 * tp] = o2s[0, own_rows, :]
    for d in range(1, 8):
        hidden_y(d).wait_send()
    for d in range(1, NX):
        hidden_x(d, x_rows).wait_send()
    for wait in sent[:-1]:
        wait()
    plane_arrived()
    result = p7[0].astype(F32)
    for b in range(1, 16):
        result = result + p7[b].astype(F32)
    out_ref[...] = result
    sent[-1]()


def per_device(hidden_in, w_query, w_key, w_value, w_out, cache_keys, cache_values, prefix_lengths):
    dma = pltpu.SemaphoreType.DMA
    vmem = pltpu.VMEM
    in_hbm = pl.BlockSpec(memory_space=pltpu.HBM)
    return pl.pallas_call(
        kernel,
        out_shape=jax.ShapeDtypeStruct((32, 128), F32),
        in_specs=[in_hbm] * 7 + [pl.BlockSpec(memory_space=pltpu.SMEM)],
        out_specs=pl.BlockSpec(memory_space=pltpu.VMEM),
        scratch_shapes=[
            vmem((256, 512), BF16), vmem((128, 1024), BF16), vmem((2, 128, 128), BF16), vmem((1024, 128), BF16),
            vmem((4, 128, 256), BF16), vmem((4, 128, 128), BF16), vmem((2, 256, 256), BF16),
            vmem((4, 512, 128), BF16), vmem((4, 512, 128), BF16),
            vmem((2, 256, 128), F32), vmem((256, 128), F32), vmem((256, 128), F32),
            vmem((16, 128), F32), vmem((16, 128), F32), vmem((8, 128), F32),
            vmem((8, 32, 128), F32), vmem((8, 32, 128), F32), vmem((8, 16, 128), F32), vmem((8, 16, 128), F32),
            vmem((2, 256, 128), BF16), vmem((4, 16, 128), F32),
            vmem((2, 8, 32, 128), BF16), vmem((2, 8, 32, 128), BF16),
            vmem((2, 8, 128), F32), vmem((2, 8, 128), F32),
            vmem((2, 256, 256), BF16), vmem((2, 256, 128), BF16), vmem((16, 32, 128), BF16),
            dma((7,)), dma((len(GROUPS),)), dma((len(GROUPS),)), dma((8,)), dma((8,)), dma((4,)), dma((4,)),
            pltpu.SemaphoreType.REGULAR((5,)),
        ],
        compiler_params=pltpu.CompilerParams(
            collective_id=0, has_side_effects=True, vmem_limit_bytes=56 * 1024 * 1024
        ),
        cost_estimate=pl.CostEstimate(flops=1_000_000_000, bytes_accessed=2_000_000, transcendentals=1_100_000),
        name="attention_block",
    )(
        hidden_in, w_query, w_key, w_value, w_out,
        cache_keys.reshape(cache_keys.shape[0], 128), cache_values.reshape(cache_values.shape[0], 128),
        prefix_lengths,
    )


def solution(mesh):
    placed = (
        P("tp", "ctx"),
        P("ctx", "tp"),
        P("ctx", "tp"),
        P("ctx", "tp"),
        P("tp", "ctx"),
        P("ctx", "tp", None),
        P("ctx", "tp", None),
        P("ctx"),
    )
    return jax.shard_map(
        per_device, mesh=mesh, in_specs=placed, out_specs=P("tp", "ctx"), check_vma=False
    )
```

```python
import functools
import math

import jax
import jax.numpy as jnp
from jax import lax
from jax.experimental import pallas as pl
from jax.experimental.pallas import tpu as pltpu
from jax.sharding import PartitionSpec as P

MESH = pl.DeviceIdType.MESH
F32 = jnp.float32
BF16 = jnp.bfloat16
NZ, NY, NX, NH = 8, 4, 4, 2
LOG2E = 1.0 / math.log(2.0)
NEG = -1e30
KEYS_WITH = 1
HEADS_WITH = 2
GROUPS = (
    "query weights", "kv weights", "cache twin", "cache line", "cache relay", "length twin", "length line",
    "length relay", "out weights", "pair",
    "queries", "kv pair", "kv", "heads 0", "heads 1", "messages", "partials 0", "partials 1", "levels 0", "levels 1", "attended", "across",
    "plane",
)


def coords():
    c = lax.axis_index("ctx")
    t = lax.axis_index("tp")
    return c // 8, (c // 2) % 4, c % 2, t // 2, t % 2


def device(z, y, core, x, h):
    return ((z * NY + y) * 2 + core, x * NH + h)


def dot(a, b):
    return jnp.dot(a, b, preferred_element_type=F32)


def dot_t(a, b):
    return lax.dot_general(a, b, (((1,), (1,)), ((), ())), preferred_element_type=F32)


def kernel(
    hid_ref, wq_ref, wk_ref, wv_ref, wo_ref, ck_ref, cv_ref, len_ref, out_ref,
    hs, wqs, wkvs, wos, wq, wkv, wo, kb, vb, yp, yin, yk, kvs, kvin, fill, p2s, p2d, p2k, p2e, qb, msgs,
    po, pod, pl_s, pl_d, att, o2s, p7, loc, ssem, rsem, s_hy, r_hy, s_hx, r_hx, known,
):
    z, y, core, x, h = coords()
    other = 1 - core
    yf = h * NY + y
    tp = x * NH + h
    own_rows = pl.ds(pl.multiple_of(tp * 32, 32), 32)
    own_cols = pl.ds(pl.multiple_of(y * 128, 128), 128)
    zrows = pl.ds(pl.multiple_of(z * 32, 32), 32)

    def xor_y(bits):
        if bits == 1:
            return y + 1 - 2 * (y % 2)
        return lax.rem(y + 2, NY)

    keys_y, heads_y = xor_y(KEYS_WITH), xor_y(HEADS_WITH)
    twin = device(z, y, other, x, h)

    def remote(src, dst, ssem, rsem, dev):
        return pltpu.make_async_remote_copy(
            src_ref=src, dst_ref=dst, send_sem=ssem, recv_sem=rsem, device_id=dev, device_id_type=MESH
        )

    sent = []

    def group(name, size):
        index = GROUPS.index(name)

        def put(src, dst, dev):
            remote(src, dst, ssem.at[index], rsem.at[index], dev).start()

        def arrived():
            remote(size, size, ssem.at[index], rsem.at[index], twin).wait_recv()

        sent.append(lambda: remote(size, size, ssem.at[index], rsem.at[index], twin).wait_send())
        return put, arrived

    local = [
        pltpu.make_async_copy(hid_ref, hs.at[own_rows, own_cols], loc.at[0]),
        pltpu.make_async_copy(wq_ref, wqs, loc.at[1]),
        pltpu.make_async_copy(wk_ref, wkvs.at[0], loc.at[2]),
        pltpu.make_async_copy(wv_ref, wkvs.at[1], loc.at[3]),
        pltpu.make_async_copy(ck_ref, kb.at[0], loc.at[4]),
        pltpu.make_async_copy(cv_ref, vb.at[0], loc.at[5]),
        pltpu.make_async_copy(wo_ref, wos, loc.at[6]),
    ]
    barrier = pltpu.get_barrier_semaphore()

    def zdev(d, at_y=y):
        to = lax.rem(z + d, NZ)
        return to, device(to, at_y, core, x, h)

    def yring(d):
        to = lax.rem(yf + d, 8)
        return device(z, to % 4, core, x, to // 4)

    near = [yring(d) for d in (4, 3, 5, 2, 6, 1, 7)]
    near += [device(z, y, core, lax.rem(x + d, NX), h) for d in (2, 1, 3)]
    near += [zdev(1)[1], zdev(7)[1], twin]
    for dev in near:
        pl.semaphore_signal(barrier, inc=1, device_id=dev, device_id_type=MESH)
    for copy in local:
        copy.start()
    pl.semaphore_wait(barrier, len(near))

    def tell(i, d):
        pl.semaphore_signal(known.at[i], inc=1, device_id=zdev(d)[1], device_id_type=MESH)

    def block(d):
        at = lax.rem(yf + 8 - d, 8)
        rows = pl.ds(pl.multiple_of((x * NH + at // 4) * 32, 32), 32)
        return hs.at[rows, pl.ds(pl.multiple_of((at % 4) * 128, 128), 128)]

    def hidden_y(d):
        return remote(block(0), block(0), s_hy.at[d], r_hy.at[d], yring(d))

    def hidden_x(d, view):
        return remote(view, view, s_hx.at[d], r_hx.at[d], device(z, y, core, lax.rem(x + d, NX), h))

    def forward(d):
        for dx in (2, 1, 3):
            hidden_x(dx, block(d)).start()

    x_rows = hs.at[pl.ds(pl.multiple_of(x * 64, 64), 64)]
    local[0].wait()
    for d in (4, 3, 5, 2, 6, 1, 7):
        hidden_y(d).start()
    forward(0)
    tell(0, 1)
    tell(1, 7)

    put, query_weights_arrived = group("query weights", wq.at[0:3])
    local[1].wait()
    for d in (2, 3, 1):
        to = lax.rem(y + d, NY)
        put(wqs.at[:, pl.ds(pl.multiple_of(to * 256, 256), 256)], wq.at[y], device(z, to, core, x, h))
    wq[y] = wqs[:, pl.ds(pl.multiple_of(y * 256, 256), 256)]

    fill[0:1, :] = jnp.full((1, 128), len_ref[0].astype(F32), F32)
    put, length_twin_arrived = group("length twin", fill.at[0:1])
    put(fill.at[0:1], fill.at[1:2], twin)
    put, cache_twin_arrived = group("cache twin", kb.at[0:2])
    for i, buf in enumerate((kb, vb)):
        local[4 + i].wait()
        put(buf.at[0], buf.at[1], twin)

    for d in (1, 7, 2, 6):
        hidden_y(d).wait_recv()
        forward(d)
    for copy in local[2:4]:
        copy.wait()
    put, kv_weights_arrived = group("kv weights", wkv.at[0:3])
    for d in (2, 3, 1):
        to = lax.rem(y + d, NY)
        put(wkvs.at[to % 2], wkv.at[y], device(z, to, core, x, h))
    wkv[y] = wkvs[y % 2]
    for i in range(2):
        pl.semaphore_wait(known.at[i], 1)
    tell(2, 1)
    tell(3, 7)
    tell(4, 2)
    for d in (3, 5, 4):
        hidden_y(d).wait_recv()
        forward(d)

    put, length_line_arrived = group("length line", fill.at[0:1])
    put(fill.at[0:1], fill.at[2:3], device(z, keys_y, core, x, h))
    put, cache_line_arrived = group("cache line", kb.at[0:2])
    for buf in (kb, vb):
        put(buf.at[0], buf.at[2], device(z, keys_y, core, x, h))

    query_weights_arrived()
    put, out_weights_arrived = group("out weights", wo.at[0])
    local[6].wait()
    for pair_core in range(2):
        for chip in range(2):
            def rows_of(at):
                return pl.ds(pl.multiple_of((at // 2) * 512 + 256 * chip + 128 * pair_core, 128), 128)

            there = wo.at[pair_core, pl.ds(128 * chip, 128)]
            put(wos.at[rows_of(heads_y)], there.at[:, pl.ds(128, 128)], device(z, heads_y, core, x, h))
            wo[pair_core, 128 * chip : 128 * chip + 128, 0:128] = wos[rows_of(y), :]

    wqf = wq[...].reshape(512, 256)

    def project(block):
        rows = pl.ds(pl.multiple_of(block * 64, 64), 64)
        both = dot(hs[rows, :], wqf)
        yp[0, rows, :] = both[:, :128]
        yp[1, rows, :] = both[:, 128:]

    project(x)
    for d in (1, 3, 2):
        hidden_x(d, x_rows).wait_recv()
        project(lax.rem(x + NX - d, NX))

    put, pair_arrived = group("pair", yin)
    put(yp.at[other], yin, twin)

    pair_arrived()
    for b in range(NZ):
        rows = slice(32 * b, 32 * b + 32)
        p2s[b] = yp[core, rows, :] + yin[rows, :]

    for i in range(2, 5):
        pl.semaphore_wait(known.at[i], 1)
    put, queries_arrived = group("queries", p2d.at[0:7])
    for d in (4, 3, 5, 2, 6, 1, 7):
        to, dev = zdev(d)
        put(p2s.at[to], p2d.at[z], dev)
    p2d[z] = p2s[z]

    kv_weights_arrived()
    yk[...] = dot(hs[...], wkv[...].reshape(512, 128))
    half = 16 * (y // 2)
    for b in range(NZ):
        p2k[b] = yk[pl.ds(pl.multiple_of(32 * b + half, 16), 16), :]
    put, kv_arrived = group("kv", p2e.at[0:7])
    for d in (4, 3, 5, 2, 6, 1, 7):
        to, dev = zdev(d)
        put(p2k.at[to], p2e.at[z], dev)
    p2e[z] = p2k[z]

    queries_arrived()
    total = p2d[0]
    for b in range(1, NZ):
        total = total + p2d[b]
    qb[0, zrows, :] = total.astype(BF16)
    put0, heads0_arrived = group("heads 0", qb.at[0, 0:224])
    put1, heads1_arrived = group("heads 1", qb.at[1])
    for d in (4, 3, 5, 2, 6, 1, 7, 0):
        put1(qb.at[0, zrows], qb.at[1, zrows], zdev(d, heads_y)[1])
    for d in (4, 3, 5, 2, 6, 1, 7):
        put0(qb.at[0, zrows], qb.at[0, zrows], zdev(d)[1])

    kv_arrived()
    total = p2e[0]
    for b in range(1, NZ):
        total = total + p2e[b]
    kvs[...] = total
    put, kv_pair_arrived = group("kv pair", kvs)
    put(kvs, kvin, twin)
    kv_pair_arrived()
    msgs[y] = total + kvin[...]
    put, messages_arrived = group("messages", msgs.at[0:3])
    for d in (2, 3, 1):
        put(msgs.at[y], msgs.at[y], device(z, lax.rem(y + d, NY), core, x, h))

    cache_line_arrived()
    length_line_arrived()
    put, length_relay_arrived = group("length relay", fill.at[0:1])
    put(fill.at[2:3], fill.at[3:4], twin)
    put, cache_relay_arrived = group("cache relay", kb.at[0:2])
    for buf in (kb, vb):
        put(buf.at[2], buf.at[3], twin)
    length_twin_arrived()
    cache_twin_arrived()
    length_relay_arrived()
    cache_relay_arrived()

    scale = LOG2E / math.sqrt(128.0)
    place = lax.broadcasted_iota(jnp.int32, (1, 512), 1).astype(F32)
    bias = []
    for slot in range(4):
        filled = jnp.concatenate([fill[slot : slot + 1, :]] * 4, axis=1)
        bias.append(jnp.where(place < filled, 0.0, NEG))
    bias = jnp.concatenate(bias, axis=1)
    keys = kb[...].reshape(2048, 128)
    values = vb[...].reshape(2048, 128)
    diagonal = lax.broadcasted_iota(jnp.int32, (32, 128), 0) == lax.broadcasted_iota(jnp.int32, (32, 128), 1)

    def attend(j, new):
        queries = qb[j]
        scores = dot_t(queries, keys) * scale + bias
        top = jnp.max(scores, axis=1, keepdims=True)
        weight = jnp.exp2(scores - top)
        sums = jnp.sum(weight, axis=1, keepdims=True)
        mixed = dot(weight.astype(BF16), values)
        if new:
            messages_arrived()
            new_keys = jnp.concatenate([msgs[i] for i in (0, 2)], axis=0).astype(BF16)
            new_values = jnp.concatenate([msgs[i] for i in (1, 3)], axis=0).astype(BF16)
            key_at = lax.broadcasted_iota(jnp.int32, (256, 32), 1) + z * 32
            row_at = lax.broadcasted_iota(jnp.int32, (256, 32), 0)
            fresh = jnp.where(key_at <= row_at, dot_t(queries, new_keys) * scale, NEG)
            raised = jnp.maximum(top, jnp.max(fresh, axis=1, keepdims=True))
            shrink = jnp.exp2(top - raised)
            weight = jnp.exp2(fresh - raised)
            sums = sums * shrink + jnp.sum(weight, axis=1, keepdims=True)
            mixed = mixed * shrink + dot(weight.astype(BF16), new_values)
            top = raised
        shared = (mixed / sums).astype(BF16)
        level = top + jnp.log2(sums)
        for b in range(NZ):
            rows = slice(32 * b, 32 * b + 32)
            po[j, b] = shared[rows]
            line = jnp.sum(jnp.where(diagonal, level[rows], 0.0), axis=0, keepdims=True)
            pl_s[j, b : b + 1, :] = line

    put0, partials0_arrived = group("partials 0", pod.at[0, 0:7])
    put1, partials1_arrived = group("partials 1", pod.at[1])
    putl0, levels0_arrived = group("levels 0", pl_d.at[0, 0:7])
    putl1, levels1_arrived = group("levels 1", pl_d.at[1])
    heads1_arrived()
    attend(1, False)
    for d in (4, 3, 5, 2, 6, 1, 7, 0):
        to, dev = zdev(d, heads_y)
        putl1(pl_s.at[1, pl.ds(to, 1)], pl_d.at[1, pl.ds(z, 1)], dev)
        put1(po.at[1, to], pod.at[1, z], dev)
    heads0_arrived()
    attend(0, True)
    for d in (4, 3, 5, 2, 6, 1, 7):
        to, dev = zdev(d)
        putl0(pl_s.at[0, pl.ds(to, 1)], pl_d.at[0, pl.ds(z, 1)], dev)
        put0(po.at[0, to], pod.at[0, z], dev)
    pod[0, z] = po[0, z]
    pl_d[0, pl.ds(z, 1), :] = pl_s[0, pl.ds(z, 1), :]
    for arrived in (partials0_arrived, levels0_arrived, partials1_arrived, levels1_arrived):
        arrived()

    levels, parts = [], []
    for j in range(2):
        for b in range(NZ):
            spread = jnp.where(diagonal, jnp.broadcast_to(pl_d[j, b : b + 1, :], (32, 128)), 0.0)
            levels.append(jnp.sum(spread, axis=1, keepdims=True))
            parts.append(pod[j, b].astype(F32))
    top = functools.reduce(jnp.maximum, levels)
    shares = [jnp.exp2(one - top) for one in levels]
    whole = functools.reduce(jnp.add, shares)
    merged = functools.reduce(jnp.add, [part * share for part, share in zip(parts, shares)])

    own_lanes = pl.ds(pl.multiple_of((y % 2) * 128, 128), 128)
    att[0, zrows, own_lanes] = (merged / whole).astype(BF16)
    put, attended_arrived = group("attended", att.at[0, 0:240])
    attended = att.at[0, zrows, own_lanes]
    for d in (4, 3, 5, 2, 6, 1, 7, 0):
        put(attended, attended, zdev(d, keys_y)[1])
    for d in (4, 3, 5, 2, 6, 1, 7):
        put(attended, attended, zdev(d)[1])
    out_weights_arrived()
    attended_arrived()
    put, across_arrived = group("across", att.at[1])
    put(att.at[0], att.at[1], twin)

    first = dot(att[0], wo[core])
    across_arrived()
    put, plane_arrived = group("plane", p7.at[0:15])
    both = (first + dot(att[1], wo[other])).astype(BF16)
    o2s[0] = both[:, :128]
    o2s[1] = both[:, 128:]
    for e, dh in ((0, 1), (1, 1), (1, 0), (0, 0)):
        for dx in (2, 1, 3, 0):
            if (e, dh, dx) == (0, 0, 0):
                continue
            to_x, to_h = lax.rem(x + dx, NX), lax.rem(h + dh, NH)
            rows = pl.ds(pl.multiple_of((to_x * NH + to_h) * 32, 32), 32)
            put(o2s.at[e, rows], p7.at[2 * tp + e], device(z, (y, heads_y)[e], core, to_x, to_h))
    p7[2 * tp] = o2s[0, own_rows, :]
    for d in range(1, 8):
        hidden_y(d).wait_send()
    for d in range(1, NX):
        hidden_x(d, x_rows).wait_send()
    for wait in sent[:-1]:
        wait()
    plane_arrived()
    result = p7[0].astype(F32)
    for b in range(1, 16):
        result = result + p7[b].astype(F32)
    out_ref[...] = result
    sent[-1]()


def per_device(hidden_in, w_query, w_key, w_value, w_out, cache_keys, cache_values, prefix_lengths):
    dma = pltpu.SemaphoreType.DMA
    vmem = pltpu.VMEM
    in_hbm = pl.BlockSpec(memory_space=pltpu.HBM)
    return pl.pallas_call(
        kernel,
        out_shape=jax.ShapeDtypeStruct((32, 128), F32),
        in_specs=[in_hbm] * 7 + [pl.BlockSpec(memory_space=pltpu.SMEM)],
        out_specs=pl.BlockSpec(memory_space=pltpu.VMEM),
        scratch_shapes=[
            vmem((256, 512), BF16), vmem((128, 1024), BF16), vmem((2, 128, 128), BF16), vmem((1024, 128), BF16),
            vmem((4, 128, 256), BF16), vmem((4, 128, 128), BF16), vmem((2, 256, 256), BF16),
            vmem((4, 512, 128), BF16), vmem((4, 512, 128), BF16),
            vmem((2, 256, 128), F32), vmem((256, 128), F32), vmem((256, 128), F32),
            vmem((16, 128), F32), vmem((16, 128), F32), vmem((8, 128), F32),
            vmem((8, 32, 128), F32), vmem((8, 32, 128), F32), vmem((8, 16, 128), F32), vmem((8, 16, 128), F32),
            vmem((2, 256, 128), BF16), vmem((4, 16, 128), F32),
            vmem((2, 8, 32, 128), BF16), vmem((2, 8, 32, 128), BF16),
            vmem((2, 8, 128), F32), vmem((2, 8, 128), F32),
            vmem((2, 256, 256), BF16), vmem((2, 256, 128), BF16), vmem((16, 32, 128), BF16),
            dma((7,)), dma((len(GROUPS),)), dma((len(GROUPS),)), dma((8,)), dma((8,)), dma((4,)), dma((4,)),
            pltpu.SemaphoreType.REGULAR((5,)),
        ],
        compiler_params=pltpu.CompilerParams(
            collective_id=0, has_side_effects=True, vmem_limit_bytes=56 * 1024 * 1024
        ),
        cost_estimate=pl.CostEstimate(flops=1_000_000_000, bytes_accessed=2_000_000, transcendentals=1_100_000),
        name="attention_block",
    )(
        hidden_in, w_query, w_key, w_value, w_out,
        cache_keys.reshape(cache_keys.shape[0], 128), cache_values.reshape(cache_values.shape[0], 128),
        prefix_lengths,
    )


def solution(mesh):
    placed = (
        P("tp", "ctx"),
        P("ctx", "tp"),
        P("ctx", "tp"),
        P("ctx", "tp"),
        P("tp", "ctx"),
        P("ctx", "tp", None),
        P("ctx", "tp", None),
        P("ctx"),
    )
    return jax.shard_map(
        per_device, mesh=mesh, in_specs=placed, out_specs=P("tp", "ctx"), check_vma=False
    )
```
